512 devices in a mesh: row: 32 (over x_hi, y, core), col: 16 (over z, x_lo).
Axes of the slice: x: 4 (x_hi: 2, x_lo: 2; x = x_hi * 2 + x_lo), y: 8, z: 8, core: 2. Of those that a mesh axis runs over, the one named last changes fastest.
Arguments:
- front_rows: bfloat16 [512, 128, 512], P('row', 'col'), may hold values from -0.0546875 to 0.0546875
- slot_blocks: int32 [512], P('row'), may hold values from -1 to 95, as said below
- inv_factor: float32 [512, 512], replicated
- ancestor_inv: float32 [12288, 12288], P('row', 'col'), may hold values from -6 to 6
Outputs:
- offdiag_inv: float32 [12288, 512], P(('row', 'col'))
- diag_inv: float32 [512, 512], P('col')
The draws below stay inside these ranges and needn't reach their ends.
Inputs may be any that keep to these rules, and one draw needn't show every extreme that they name: `slot_blocks`: each of the 96 blocks stands in exactly one slot and -1 marks an empty slot. Block b belongs to column panel b // 6; the 16 slots of one row index hold at most 1 block of one panel, and some row index holds exactly 1 block of every panel.
All inputs are finite; a program needn't handle non-finite values.
Results may differ from the reference program's by a relative error of at most 0.0041.
Values may be sent and summed in bfloat16 or wider, within the bound.
No kernel may reach another device: no remote copies, remote signals or barrier semaphores. Data moves between devices by JAX's collectives and lax.ppermute only.
A program may use at most 64 MiB of HBM per device.

```python
import math
import jax
import jax.numpy as jnp
from jax import lax

W = 512
BLK = 128
TILE_ROWS = 384
M = 12288
PANEL_ROWS = 768
PANEL_BLOCKS = 6
CAND = 1
SLOTS = 16
N_ROW = 32
N_COL = 16


def draw_slot_blocks(key, part):
    row_count = M // TILE_ROWS
    col_count = SLOTS // CAND
    subkeys = jax.random.split(key, 5)
    full_row = jax.random.randint(subkeys[0], (), 0, row_count)
    weight = jax.random.randint(subkeys[1], (row_count,), 0, 8)
    spot_count = row_count * CAND
    spot_row = jnp.arange(spot_count) // CAND
    raw_scores = jax.random.randint(subkeys[2], (col_count, spot_count), 0, 4096)
    scores = raw_scores // (1 + weight[spot_row])[None, :] * spot_count + jnp.arange(spot_count)[None, :]
    scores = jnp.where(spot_row[None, :] == full_row, 4096 * spot_count + spot_count, scores)
    ranked = jnp.argsort(scores, axis=1)
    remaining = PANEL_BLOCKS - CAND
    chosen = ranked[:, :remaining]
    shuffle = jnp.argsort(jax.random.randint(subkeys[3], (col_count, PANEL_BLOCKS), 0, 65536) * PANEL_BLOCKS + jnp.arange(PANEL_BLOCKS)[None, :], axis=1)
    block_ids = (shuffle + (jnp.arange(col_count) * PANEL_BLOCKS)[:, None]).astype(jnp.int32)
    full_spots = full_row * CAND + jnp.arange(CAND)
    panel_iota = jnp.arange(col_count)[:, None]
    slot_table = jnp.full((col_count, spot_count), -1, jnp.int32)
    slot_table = slot_table.at[panel_iota, full_spots[None, :]].set(block_ids[:, :CAND])
    slot_table = slot_table.at[panel_iota, chosen].set(block_ids[:, CAND:])
    slot_table = slot_table.reshape(col_count, row_count, CAND).transpose(1, 0, 2).reshape(row_count, SLOTS)
    mixing = jax.random.randint(subkeys[4], (row_count, SLOTS), 0, 65536) * SLOTS + jnp.arange(SLOTS)[None, :]
    shuffle_rows = jnp.argsort(mixing, axis=1)
    slot_table = jnp.take_along_axis(slot_table, shuffle_rows, axis=1)
    return slot_table.reshape(-1).astype(jnp.int32)


def draw_inv_factor(key, part):
    first_key, second_key = jax.random.split(key)
    lower_part = jax.random.normal(first_key, (W, W), jnp.float32) / math.sqrt(W)
    diagonal_part = jax.random.uniform(second_key, (W,), jnp.float32, 1.0, 2.0)
    return jnp.tril(lower_part, -1) + jnp.diag(diagonal_part)


def spiked(values, own_key, source, target, blocks, factor):
    owner, partner = [(jnp.arange(values.shape[position]) // (values.shape[position] // blocks)).reshape([-1 if axis == position else 1 for axis in range(values.ndim)]) for position in (source, target)]
    chosen = jax.random.permutation(own_key, blocks)[partner]
    strong = (owner == chosen) | (owner == (partner + blocks // 2) % blocks)
    return jnp.where(strong, factor * values, values)


def steps_of(own_key, extent, shards, least, top_value):
    loudness, own = 1.0, jax.random.fold_in(own_key, 6)
    for dim, parts in shards:
        draws = jnp.exp(jax.random.uniform(jax.random.fold_in(own, dim), (parts,), jnp.float32, least / len(shards), top_value / len(shards)))
        loudness = loudness * jnp.repeat(draws, extent[dim] // parts).reshape([-1 if axis == dim else 1 for axis in range(len(extent))])
    return loudness


def centred(key, dims, spread, limit, shards=(), kind=jnp.bfloat16):
    drawn = spread * jax.random.normal(key, dims, jnp.float32)
    if shards:
        drawn = drawn * steps_of(key, dims, shards, -0.22, 0.18)
    return jnp.clip(drawn, -limit, limit).astype(kind)


def gaussian_with(stream_key, dims, deviation, reach, cuts, heavy, dtype=jnp.bfloat16):
    result = deviation * jax.random.normal(stream_key, dims, jnp.float32)
    if cuts:
        result = result * steps_of(stream_key, dims, cuts, -0.22, 0.18)
    return jnp.clip(spiked(result, jax.random.fold_in(stream_key, 3), *heavy), -reach, reach).astype(dtype)


def setup_inputs(seed: int = 0) -> dict:
    key_of = jax.random.split(jax.random.key(seed), 5)
    front_rows = centred(key_of[0], (N_ROW * SLOTS, BLK, W), M ** -0.5, 0.0546875, ((0, 32), (1, 16)))
    slot_blocks = draw_slot_blocks(jax.random.fold_in(key_of[4], 71), 0)
    inv_factor = draw_inv_factor(jax.random.fold_in(key_of[4], 71), 0)
    ancestor_inv = gaussian_with(key_of[3], (M, PANEL_ROWS * N_COL), 1.0, 6.0, ((0, 32), (1, 16)), (1, 0, 32, 2.75), jnp.float32)
    return dict(front_rows=front_rows, slot_blocks=slot_blocks, inv_factor=inv_factor, ancestor_inv=ancestor_inv)


def reference(front_rows, slot_blocks, inv_factor, ancestor_inv):
    nblocks = M // BLK
    target_rows = jnp.where(slot_blocks >= 0, slot_blocks, nblocks).astype(jnp.int32)
    placed = jnp.zeros((nblocks + 1, BLK, W), jnp.bfloat16).at[target_rows].set(front_rows)[:nblocks]
    lower_rows = placed.reshape(M, W).astype(jnp.float32)
    scaled = jnp.dot(lower_rows, inv_factor, precision=lax.Precision.HIGHEST, preferred_element_type=jnp.float32).astype(jnp.bfloat16)
    scaled_full = scaled.astype(jnp.float32)
    product = jnp.dot(ancestor_inv, scaled_full, precision=lax.Precision.HIGHEST, preferred_element_type=jnp.float32)
    gram_total = jnp.dot(scaled_full.T, product, precision=lax.Precision.HIGHEST, preferred_element_type=jnp.float32)
    factor_gram = jnp.dot(inv_factor.T, inv_factor, precision=lax.Precision.HIGHEST, preferred_element_type=jnp.float32)
    return -product, factor_gram + gram_total
```

```python
import jax
import jax.numpy as jnp
from jax import lax
from jax.sharding import PartitionSpec as P

BF16 = jnp.bfloat16
F32 = jnp.float32


def body(front_rows, slot_blocks, inv_factor, ancestor_inv):
    col_count = lax.axis_size("col")
    row_count = lax.axis_size("row")
    chip_count = row_count // 2
    col_index = lax.axis_index("col")
    row_index = lax.axis_index("row")
    core = row_index % 2
    slot_count, chunk_rows, width = front_rows.shape
    half = width // 2
    tile_rows, panel_rows = ancestor_inv.shape
    block_rows = chunk_rows * col_count
    panel_blocks = panel_rows // block_rows
    same_core = [[2 * j + k for j in range(chip_count)] for k in range(2)]
    core_pairs = [[2 * j, 2 * j + 1] for j in range(chip_count)]
    core_swap = [(i, i ^ 1) for i in range(row_count)]

    scaled = jnp.dot(
        front_rows.reshape(slot_count * chunk_rows, width).astype(F32),
        inv_factor,
        precision=lax.Precision.HIGHEST,
        preferred_element_type=F32,
    ).astype(BF16)
    slot_panel = jnp.where(slot_blocks >= 0, slot_blocks // panel_blocks, -1)
    panels = jnp.arange(col_count, dtype=jnp.int32)
    chosen = slot_panel[None, :] == panels[:, None]
    by_panel = jnp.einsum(
        "ps,sbw->pbw",
        chosen.astype(BF16),
        scaled.reshape(slot_count, chunk_rows, width),
        preferred_element_type=F32,
    ).astype(BF16)
    mine = slot_panel == col_index
    offset = jnp.sum(jnp.where(mine, slot_blocks % panel_blocks + 1, 0)) - 1

    block = lax.all_to_all(by_panel, "col", 0, 0, tiled=True)
    dealt = block.reshape(chip_count, chunk_rows, 2, half).transpose(0, 2, 1, 3)
    dealt = dealt.reshape(row_count, chunk_rows, half)
    tag = jnp.full((row_count, chunk_rows, 128), offset.astype(BF16), BF16)
    taken = lax.all_to_all(jnp.concatenate([dealt, tag], 2), "row", 0, 0, tiled=True)
    numbers = taken[:, 0, half].astype(F32)
    place = numbers[None, :] == jnp.arange(panel_blocks, dtype=F32)[:, None]
    piece = jnp.einsum(
        "os,sbw->obw", place.astype(BF16), taken[:, :, :half], preferred_element_type=F32
    ).astype(BF16)

    copies = jnp.broadcast_to(piece[None], (chip_count, *piece.shape))
    parts = lax.all_to_all(copies, "row", 0, 0, tiled=True, axis_index_groups=same_core)
    own_half = parts.transpose(1, 0, 2, 3).reshape(panel_rows, half)
    other_half = lax.ppermute(own_half, "row", core_swap)

    tile = ancestor_inv.astype(BF16)
    own_sum = jnp.dot(tile, own_half, preferred_element_type=F32)
    other_sum = jnp.dot(tile, other_half, preferred_element_type=F32)

    def both(own, other):
        return jnp.where(
            core == 0, jnp.concatenate([own, other], 1), jnp.concatenate([other, own], 1)
        )

    share = tile_rows // col_count
    start = row_index * share
    share_rows = both(
        lax.dynamic_slice_in_dim(own_half, start, share, 0),
        lax.dynamic_slice_in_dim(other_half, start, share, 0),
    )
    route = [
        (r * col_count + p, (2 * p + r // col_count) * col_count + r % col_count)
        for r in range(row_count)
        for p in range(col_count)
    ]
    own_factor = lax.ppermute(share_rows, ("row", "col"), route)

    partial_sums = both(own_sum, other_sum).astype(BF16).reshape(col_count, share, width)
    arrived = lax.all_to_all(partial_sums, "col", 0, 0, tiled=True)
    column_total = jnp.sum(arrived.astype(F32), axis=0)

    pair_total = lax.all_gather(column_total, "row", axis=0, tiled=True, axis_index_groups=core_pairs)
    pair_factor = lax.all_gather(own_factor, "row", axis=0, tiled=True, axis_index_groups=core_pairs)
    gram_part = lax.dot_general(
        pair_factor,
        pair_total.astype(BF16),
        (((0,), (0,)), ((), ())),
        preferred_element_type=F32,
    )
    diag_width = width // col_count
    gram_half = lax.dynamic_index_in_dim(
        gram_part.reshape(col_count, 2, diag_width // 2, width), core, 1, keepdims=False
    ).astype(BF16)
    gram_piece = jnp.sum(lax.all_to_all(gram_half, "col", 0, 0, tiled=True).astype(F32), axis=0)
    copies = jnp.broadcast_to(gram_piece.astype(BF16)[None], (chip_count, *gram_piece.shape))
    pieces = lax.all_to_all(copies, "row", 0, 0, tiled=True, axis_index_groups=same_core)
    gram_rows = jnp.sum(pieces.astype(F32), axis=0)
    gram_block = lax.all_gather(gram_rows, "row", axis=0, tiled=True, axis_index_groups=core_pairs)
    factor_cols = lax.dynamic_slice_in_dim(inv_factor, col_index * diag_width, diag_width, 1)
    factor_gram = lax.dot_general(
        factor_cols,
        inv_factor,
        (((0,), (0,)), ((), ())),
        precision=lax.Precision.HIGHEST,
        preferred_element_type=F32,
    )
    return (-column_total, factor_gram + gram_block)


def solution(mesh):
    in_specs = (P("row", "col", None), P("row"), P(), P("row", "col"))
    out_specs = (P(("row", "col"), None), P("col", None))
    return jax.shard_map(body, mesh=mesh, in_specs=in_specs, out_specs=out_specs, check_vma=False)
```

```python
import jax
import jax.numpy as jnp
from jax import lax
from jax.experimental import pallas as pl
from jax.experimental.pallas import tpu as pltpu
from jax.sharding import PartitionSpec as P

BF16 = jnp.bfloat16
F32 = jnp.float32
TAG = 128
SMEM = pl.BlockSpec(memory_space=pltpu.SMEM)
VMEM = pl.BlockSpec(memory_space=pltpu.VMEM)
PARAMS = pltpu.CompilerParams(vmem_limit_bytes=16 * 2**20)


def dot(a, b, dims=((1,), (0,))):
    return lax.dot_general(a, b, (dims, ((), ())), preferred_element_type=F32)


def split(x):
    high = x.astype(BF16)
    return high, (x - high.astype(F32)).astype(BF16)


def by_core(shape, natural, group):
    column = lax.broadcasted_iota(jnp.int32, shape, natural)
    place = lax.broadcasted_iota(jnp.int32, shape, 1 - natural)
    part = group // 2
    core = (column % group) // part
    target = core * (shape[natural] // 2) + (column // group) * part + column % part
    return jnp.where(target == place, 1.0, 0.0).astype(BF16)


def scale_kernel(panel_blocks, group, slots_ref, rows_ref, factor_ref, out_ref, scaled_ref):
    width = factor_ref.shape[1]
    high, low = split(factor_ref[...])
    rows = rows_ref[...]
    scaled = (dot(rows, high) + dot(rows, low)).astype(BF16)
    scaled_ref[...] = dot(scaled, by_core((width, width), 0, group))
    out_ref[...] = jnp.zeros_like(out_ref)
    slot_count = slots_ref.shape[0]
    height = rows_ref.shape[0] // slot_count
    for s in range(slot_count):
        block = slots_ref[s]

        @pl.when(block >= 0)
        def _():
            panel = block // panel_blocks
            number = (block - panel * panel_blocks + 1).astype(F32)
            out_ref[panel, :, :width] = scaled_ref[s * height : (s + 1) * height, :].astype(BF16)
            out_ref[panel, :, width:] = jnp.full((height, TAG), number, F32).astype(BF16)


def place_kernel(taken_ref, out_ref):
    width = taken_ref.shape[2] - TAG
    tags = [taken_ref[s, :, width:].astype(F32) for s in range(taken_ref.shape[0])]
    for lanes in range(0, width, TAG):
        values = [
            taken_ref[s, :, lanes : lanes + TAG].astype(F32) for s in range(taken_ref.shape[0])
        ]
        for number in range(out_ref.shape[0]):
            total = jnp.zeros_like(values[0])
            for tag, value in zip(tags, values):
                total = total + jnp.where(tag == number + 1, value, 0.0)
            out_ref[number, :, lanes : lanes + TAG] = total.astype(BF16)


def merge_kernel(core_ref, pair_ref, out_ref, copies_ref):
    half = out_ref.shape[2]

    def merge(first):
        for b in range(out_ref.shape[0]):
            rows = [pair_ref[k, b, :, first : first + half].astype(F32) for k in range(2)]
            rows = (rows[0] + rows[1]).astype(BF16)
            out_ref[b] = rows
            for copy in range(copies_ref.shape[0]):
                copies_ref[copy, b] = rows

    @pl.when(core_ref[0] == 0)
    def _():
        merge(0)

    @pl.when(core_ref[0] == 1)
    def _():
        merge(half)


def product_kernel(group, tile_ref, halves_ref, out_ref):
    half = halves_ref.shape[2]
    back = by_core((2 * half, 2 * half), 1, group)
    panel = dot(halves_ref[0], back[:half]) + dot(halves_ref[1], back[half:])
    panel = panel.astype(BF16)
    high, low = split(tile_ref[...])
    out_ref[...] = (dot(high, panel) + dot(low, panel)).astype(BF16)


def body(front_rows, slot_blocks, inv_factor, ancestor_inv):
    col_count = lax.axis_size("col")
    row_count = lax.axis_size("row")
    chip_count = row_count // 2
    col_index = lax.axis_index("col")
    core = lax.axis_index("row") % 2
    core_arg = jnp.reshape(core, (1,)).astype(jnp.int32)
    slot_count, chunk_rows, width = front_rows.shape
    half = width // 2
    tile_rows, panel_rows = ancestor_inv.shape
    block_rows = chunk_rows * col_count
    panel_blocks = panel_rows // block_rows
    share = tile_rows // col_count
    diag_width = width // col_count
    same_core = [[2 * j + k for j in range(chip_count)] for k in range(2)]
    core_pairs = [[2 * j, 2 * j + 1] for j in range(chip_count)]

    def pair_gather(x):
        return lax.all_gather(x, "row", axis=0, axis_index_groups=core_pairs)

    def over_row(x):
        return lax.all_to_all(x, "row", 0, 0, tiled=True, axis_index_groups=same_core)

    def over_col(x):
        return lax.all_to_all(x, "col", 0, 0, tiled=True)

    factor_cols = lax.dynamic_slice_in_dim(inv_factor, col_index * diag_width, diag_width, 1)
    factor_gram = lax.optimization_barrier(
        lax.dot_general(
            factor_cols,
            inv_factor,
            (((0,), (0,)), ((), ())),
            precision=lax.Precision.HIGHEST,
            preferred_element_type=F32,
        )
    )

    by_panel = pl.pallas_call(
        lambda *refs: scale_kernel(panel_blocks, diag_width, *refs),
        out_shape=jax.ShapeDtypeStruct((col_count, chunk_rows, width + TAG), BF16),
        in_specs=[SMEM, VMEM, VMEM],
        out_specs=VMEM,
        scratch_shapes=[pltpu.VMEM((slot_count * chunk_rows, width), F32)],
        compiler_params=PARAMS,
    )(slot_blocks, front_rows.reshape(slot_count * chunk_rows, width), inv_factor)
    placed = pl.pallas_call(
        place_kernel,
        out_shape=jax.ShapeDtypeStruct((panel_blocks, chunk_rows, width), BF16),
        in_specs=[VMEM],
        out_specs=VMEM,
        compiler_params=PARAMS,
    )(over_row(by_panel))
    piece, copies = pl.pallas_call(
        merge_kernel,
        out_shape=(
            jax.ShapeDtypeStruct((panel_blocks, chunk_rows, half), BF16),
            jax.ShapeDtypeStruct((col_count, panel_blocks, chunk_rows, half), BF16),
        ),
        in_specs=[SMEM, VMEM],
        out_specs=(VMEM, VMEM),
        compiler_params=PARAMS,
    )(core_arg, pair_gather(placed))

    route = [
        ((2 * j + k) * col_count + p, (2 * p + k) * col_count + j)
        for j in range(chip_count)
        for k in range(2)
        for p in range(col_count)
    ]
    turned = lax.ppermute(piece, ("row", "col"), route)
    pair_factor = over_col(copies).transpose(1, 0, 2, 3).reshape(2 * tile_rows, half)
    copies = jnp.broadcast_to(turned[None], (chip_count, *turned.shape))
    own_half = over_row(copies).transpose(1, 0, 2, 3).reshape(panel_rows, half)

    partial_sums = pl.pallas_call(
        lambda *refs: product_kernel(diag_width, *refs),
        out_shape=jax.ShapeDtypeStruct((tile_rows, width), BF16),
        in_specs=[VMEM, VMEM],
        out_specs=VMEM,
        compiler_params=PARAMS,
    )(ancestor_inv, pair_gather(own_half))
    pair_sums = pair_gather(partial_sums).reshape(2 * tile_rows, width)
    gram_half = dot(pair_factor, pair_sums, ((0,), (0,))).astype(BF16)
    sent = jnp.concatenate(
        [
            gram_half.reshape(col_count, diag_width // 2, width),
            partial_sums.reshape(col_count, share, width),
        ],
        1,
    )
    sums = jnp.sum(over_col(sent).astype(F32), axis=0)
    gram_piece, column_total = sums[: diag_width // 2], sums[diag_width // 2 :]
    copies = jnp.broadcast_to(gram_piece.astype(BF16)[None], (chip_count, *gram_piece.shape))
    gram_rows = jnp.sum(over_row(copies).astype(F32), axis=0)
    gram_block = pair_gather(gram_rows).reshape(diag_width, width)
    return (-column_total, factor_gram + gram_block)


def solution(mesh):
    in_specs = (P("row", "col", None), P("row"), P(), P("row", "col"))
    out_specs = (P(("row", "col"), None), P("col", None))
    return jax.shard_map(body, mesh=mesh, in_specs=in_specs, out_specs=out_specs, check_vma=False)
```

```python
import jax
import jax.numpy as jnp
from jax import lax
from jax.experimental import pallas as pl
from jax.experimental.pallas import tpu as pltpu
from jax.sharding import PartitionSpec as P

BF16 = jnp.bfloat16
F32 = jnp.float32
TAG = 128
SMEM = pl.BlockSpec(memory_space=pltpu.SMEM)
VMEM = pl.BlockSpec(memory_space=pltpu.VMEM)
PARAMS = pltpu.CompilerParams(vmem_limit_bytes=16 * 2**20)


def dot(a, b, dims=((1,), (0,))):
    return lax.dot_general(a, b, (dims, ((), ())), preferred_element_type=F32)


def split(x):
    high = x.astype(BF16)
    return high, (x - high.astype(F32)).astype(BF16)


def by_core(shape, natural, group):
    column = lax.broadcasted_iota(jnp.int32, shape, natural)
    place = lax.broadcasted_iota(jnp.int32, shape, 1 - natural)
    part = group // 2
    core = (column % group) // part
    target = core * (shape[natural] // 2) + (column // group) * part + column % part
    return jnp.where(target == place, 1.0, 0.0).astype(BF16)


def scale_kernel(panel_blocks, group, slots_ref, rows_ref, factor_ref, out_ref, scaled_ref):
    width = factor_ref.shape[1]
    high, low = split(factor_ref[...])
    rows = rows_ref[...]
    scaled = (dot(rows, high) + dot(rows, low)).astype(BF16)
    scaled_ref[...] = dot(scaled, by_core((width, width), 0, group))
    out_ref[...] = jnp.zeros_like(out_ref)
    slot_count = slots_ref.shape[0]
    height = rows_ref.shape[0] // slot_count
    for s in range(slot_count):
        block = slots_ref[s]

        @pl.when(block >= 0)
        def _():
            panel = block // panel_blocks
            number = (block - panel * panel_blocks + 1).astype(F32)
            out_ref[panel, :, :width] = scaled_ref[s * height : (s + 1) * height, :].astype(BF16)
            out_ref[panel, :, width:] = jnp.full((height, TAG), number, F32).astype(BF16)


def place_kernel(taken_ref, out_ref):
    width = taken_ref.shape[2] - TAG
    tags = [taken_ref[s, :, width:].astype(F32) for s in range(taken_ref.shape[0])]
    for lanes in range(0, width, TAG):
        values = [
            taken_ref[s, :, lanes : lanes + TAG].astype(F32) for s in range(taken_ref.shape[0])
        ]
        for number in range(out_ref.shape[0]):
            total = jnp.zeros_like(values[0])
            for tag, value in zip(tags, values):
                total = total + jnp.where(tag == number + 1, value, 0.0)
            out_ref[number, :, lanes : lanes + TAG] = total.astype(BF16)


def merge_kernel(core_ref, pair_ref, out_ref):
    half = out_ref.shape[2]

    def merge(first):
        for b in range(out_ref.shape[0]):
            rows = [pair_ref[k, b, :, first : first + half].astype(F32) for k in range(2)]
            out_ref[b] = (rows[0] + rows[1]).astype(BF16)

    @pl.when(core_ref[0] == 0)
    def _():
        merge(0)

    @pl.when(core_ref[0] == 1)
    def _():
        merge(half)


def product_kernel(group, tile_ref, halves_ref, out_ref):
    half = halves_ref.shape[2]
    back = by_core((2 * half, 2 * half), 1, group)
    panel = dot(halves_ref[0], back[:half]) + dot(halves_ref[1], back[half:])
    panel = panel.astype(BF16)
    high, low = split(tile_ref[...])
    out_ref[...] = (dot(high, panel) + dot(low, panel)).astype(BF16)


def body(front_rows, slot_blocks, inv_factor, ancestor_inv):
    col_count = lax.axis_size("col")
    row_count = lax.axis_size("row")
    chip_count = row_count // 2
    col_index = lax.axis_index("col")
    core = lax.axis_index("row") % 2
    core_arg = jnp.reshape(core, (1,)).astype(jnp.int32)
    slot_count, chunk_rows, width = front_rows.shape
    half = width // 2
    tile_rows, panel_rows = ancestor_inv.shape
    block_rows = chunk_rows * col_count
    panel_blocks = panel_rows // block_rows
    share = tile_rows // col_count
    diag_width = width // col_count
    same_core = [[2 * j + k for j in range(chip_count)] for k in range(2)]
    core_pairs = [[2 * j, 2 * j + 1] for j in range(chip_count)]

    def pair_gather(x):
        return lax.all_gather(x, "row", axis=0, axis_index_groups=core_pairs)

    def over_row(x):
        return lax.all_to_all(x, "row", 0, 0, tiled=True, axis_index_groups=same_core)

    def over_col(x):
        return lax.all_to_all(x, "col", 0, 0, tiled=True)

    factor_cols = lax.dynamic_slice_in_dim(inv_factor, col_index * diag_width, diag_width, 1)
    factor_gram = lax.optimization_barrier(
        lax.dot_general(
            factor_cols,
            inv_factor,
            (((0,), (0,)), ((), ())),
            precision=lax.Precision.HIGHEST,
            preferred_element_type=F32,
        )
    )

    by_panel = pl.pallas_call(
        lambda *refs: scale_kernel(panel_blocks, diag_width, *refs),
        out_shape=jax.ShapeDtypeStruct((col_count, chunk_rows, width + TAG), BF16),
        in_specs=[SMEM, VMEM, VMEM],
        out_specs=VMEM,
        scratch_shapes=[pltpu.VMEM((slot_count * chunk_rows, width), F32)],
        compiler_params=pltpu.CompilerParams(vmem_limit_bytes=60 * 2**20),
    )(slot_blocks, front_rows.reshape(slot_count * chunk_rows, width), inv_factor)
    placed = pl.pallas_call(
        place_kernel,
        out_shape=jax.ShapeDtypeStruct((panel_blocks, chunk_rows, width), BF16),
        in_specs=[VMEM],
        out_specs=VMEM,
        compiler_params=PARAMS,
    )(over_row(by_panel))
    piece = pl.pallas_call(
        merge_kernel,
        out_shape=jax.ShapeDtypeStruct((panel_blocks, chunk_rows, half), BF16),
        in_specs=[SMEM, VMEM],
        out_specs=VMEM,
        compiler_params=PARAMS,
    )(core_arg, pair_gather(placed))

    route = [
        ((2 * j + k) * col_count + p, (2 * p + k) * col_count + j)
        for j in range(chip_count)
        for k in range(2)
        for p in range(col_count)
    ]
    turned = lax.ppermute(piece, ("row", "col"), route)
    copies = jnp.broadcast_to(turned[None], (chip_count, *turned.shape))
    own_half = over_row(copies).transpose(1, 0, 2, 3).reshape(panel_rows, half)

    turns = share // chunk_rows
    by_tile = piece.reshape(2, turns, chunk_rows, half)
    chunks = [
        lax.ppermute(
            lax.dynamic_index_in_dim(by_tile, (t - col_index) % turns, 1, keepdims=False),
            "col",
            [((turns * d + t) % col_count, d) for d in range(col_count)],
        )
        for t in range(turns)
    ]
    pair_factor = jnp.stack(chunks, 1).reshape(2 * share, half)

    partial_sums = pl.pallas_call(
        lambda *refs: product_kernel(diag_width, *refs),
        out_shape=jax.ShapeDtypeStruct((tile_rows, width), BF16),
        in_specs=[VMEM, VMEM],
        out_specs=VMEM,
        compiler_params=PARAMS,
    )(ancestor_inv, pair_gather(own_half))
    arrived = over_col(partial_sums.reshape(col_count, share, width))
    column_total = jnp.sum(arrived.astype(F32), axis=0)

    pair_total = pair_gather(column_total).reshape(2 * share, width)
    gram_half = lax.dot_general(
        pair_factor.astype(F32),
        pair_total,
        (((0,), (0,)), ((), ())),
        precision=lax.Precision.HIGH,
        preferred_element_type=F32,
    ).astype(BF16)
    arrived = over_col(gram_half.reshape(col_count, diag_width // 2, width))
    gram_piece = jnp.sum(arrived.astype(F32), axis=0)
    copies = jnp.broadcast_to(gram_piece.astype(BF16)[None], (chip_count, *gram_piece.shape))
    gram_rows = jnp.sum(over_row(copies).astype(F32), axis=0)
    gram_block = pair_gather(gram_rows).reshape(diag_width, width)
    return (-column_total, factor_gram + gram_block)


def solution(mesh):
    in_specs = (P("row", "col", None), P("row"), P(), P("row", "col"))
    out_specs = (P(("row", "col"), None), P("col", None))
    return jax.shard_map(body, mesh=mesh, in_specs=in_specs, out_specs=out_specs, check_vma=False)
```

```python
import itertools

import jax
import jax.numpy as jnp
import numpy as np
from jax import lax
from jax.experimental import pallas as pl
from jax.experimental.pallas import tpu as pltpu
from jax.sharding import PartitionSpec as P

BF16 = jnp.bfloat16
F32 = jnp.float32
TAG = 128
SMEM = pl.BlockSpec(memory_space=pltpu.SMEM)
VMEM = pl.BlockSpec(memory_space=pltpu.VMEM)
PARAMS = pltpu.CompilerParams(vmem_limit_bytes=16 * 2**20)
FETCHING = pltpu.CompilerParams(vmem_limit_bytes=60 * 2**20)


def dot(a, b, dims=((1,), (0,))):
    return lax.dot_general(a, b, (dims, ((), ())), preferred_element_type=F32)


def split(x):
    high = x.astype(BF16)
    return high, (x - high.astype(F32)).astype(BF16)


def by_core(width, group):
    part = group // 2
    column = np.arange(width)
    target = (column % group) // part * (width // 2) + column // group * part + column % part
    matrix = np.zeros((width, width), np.float32)
    matrix[column, target] = 1.0
    return matrix


def chip_position(chip, col, chip_count):
    ys = chip_count // 2
    return chip // ys * 2 + col % 2, chip % ys, col // 2


def hops(a, b, sizes):
    return sum(min((p - q) % n, (q - p) % n) for p, q, n in zip(a, b, sizes))


def short_routes(chip_count, col_count):
    sizes = (4, chip_count // 2, col_count // 2)
    table = np.zeros((col_count, col_count), np.int32)
    for p in range(col_count):
        source = [chip_position(p, c, chip_count) for c in range(col_count)]
        target = [chip_position(j, p, chip_count) for j in range(chip_count)]
        cost = [[hops(s, t, sizes) for t in target] for s in source]
        for limit in itertools.count():
            owner = {}

            def assign(c, seen):
                for j in range(chip_count):
                    if cost[c][j] <= limit and j not in seen:
                        seen.add(j)
                        if j not in owner or assign(owner[j], seen):
                            owner[j] = c
                            return True
                return False

            if all(assign(c, set()) for c in range(col_count)):
                break
        for j, c in owner.items():
            table[p, c] = j
    return table


def scale_kernel(panel_blocks, slots_ref, rows_ref, factor_ref, order_ref, out_ref, scaled_ref):
    half = factor_ref.shape[1] // 2
    high, low = split(factor_ref[...])
    rows = rows_ref[...]
    scaled = (dot(rows, high) + dot(rows, low)).astype(BF16)
    scaled_ref[...] = dot(scaled, order_ref[...])
    out_ref[...] = jnp.zeros_like(out_ref)
    slot_count = slots_ref.shape[0]
    height = rows_ref.shape[0] // slot_count
    for s in range(slot_count):
        block = slots_ref[s]

        @pl.when(block >= 0)
        def _():
            panel = block // panel_blocks
            number = (block - panel * panel_blocks + 1).astype(F32)
            for k in range(2):
                part = scaled_ref[s * height : (s + 1) * height, k * half : (k + 1) * half]
                out_ref[2 * panel + k, :, :half] = part.astype(BF16)
                out_ref[2 * panel + k, :, half:] = jnp.full((height, TAG), number, F32).astype(BF16)


def place_kernel(taken_ref, out_ref):
    width = taken_ref.shape[2] - TAG
    sources = range(taken_ref.shape[0])
    for lanes in range(0, width, TAG):
        totals = [jnp.zeros((taken_ref.shape[1], TAG), F32) for _ in range(out_ref.shape[0])]
        for s in sources:
            tag = taken_ref[s, :, width:].astype(F32)
            value = taken_ref[s, :, lanes : lanes + TAG].astype(F32)
            totals = [t + jnp.where(tag == n + 1, value, 0.0) for n, t in enumerate(totals)]
        for n, total in enumerate(totals):
            out_ref[n, :, lanes : lanes + TAG] = total.astype(BF16)


def product_kernel(col_ref, chip_ref, tile_ref, parts_ref, piece_ref, back_ref, out_ref, panel_ref, sent_ref):
    chunks, blocks, height, half = parts_ref.shape[1:]
    share = sent_ref.shape[1] - height
    for c in range(chunks):
        for b in range(blocks):
            first = (b * chunks + c) * height
            for k in range(2):
                rows = parts_ref[k, chip_ref[c], b].astype(F32)
                panel_ref[first : first + height, k * half : (k + 1) * half] = rows
    panel = dot(panel_ref[...].astype(BF16), back_ref[...]).astype(BF16)
    high, low = split(tile_ref[...])
    sums = dot(high, panel) + dot(low, panel)
    sent_ref[:, :share, :] = sums.reshape(chunks, share, 2 * half)
    sent_ref[:, share:, :] = jnp.zeros((chunks, height, 2 * half), F32)
    for b in range(blocks // 2):
        target = (b * chunks + col_ref[0]) // (share // height)
        for h in range(2):
            rows = piece_ref[h * (blocks // 2) + b].astype(F32)
            sent_ref[target, share:, h * half : (h + 1) * half] = rows
    out_ref[...] = sent_ref[...].astype(BF16)


def total_kernel(col_ref, arrived_ref, total_ref, factor_ref):
    sources = arrived_ref.shape[0]
    share, width = total_ref.shape
    height = arrived_ref.shape[1] - share
    total = arrived_ref[0].astype(F32)
    for s in range(1, sources):
        total = total + arrived_ref[s].astype(F32)
    total_ref[...] = total[:share]
    turns = share // height
    for t in range(turns):
        rows = arrived_ref[(turns * col_ref[0] + t) % sources].astype(F32)[share:]
        for h in range(2):
            first = h * share + t * height
            factor_ref[first : first + height, :] = rows[:, h * width // 2 : (h + 1) * width // 2]


def copies_kernel(arrived_ref, out_ref):
    total = arrived_ref[0].astype(F32)
    for s in range(1, arrived_ref.shape[0]):
        total = total + arrived_ref[s].astype(F32)
    for copy in range(out_ref.shape[0]):
        out_ref[copy] = total.astype(BF16)


def body(front_rows, slot_blocks, inv_factor, ancestor_inv):
    col_count = lax.axis_size("col")
    row_count = lax.axis_size("row")
    chip_count = row_count // 2
    col_index = lax.axis_index("col")
    slot_count, chunk_rows, width = front_rows.shape
    half = width // 2
    tile_rows, panel_rows = ancestor_inv.shape
    block_rows = chunk_rows * col_count
    panel_blocks = panel_rows // block_rows
    share = tile_rows // col_count
    diag_width = width // col_count
    same_core = [[2 * j + k for j in range(chip_count)] for k in range(2)]
    core_pairs = [[2 * j, 2 * j + 1] for j in range(chip_count)]
    order = by_core(width, diag_width)
    table = short_routes(chip_count, col_count)
    col_arg = jnp.reshape(col_index, (1,)).astype(jnp.int32)
    chip_arg = lax.dynamic_index_in_dim(jnp.asarray(table), col_index, 0, keepdims=False)

    def pair_gather(x):
        return lax.all_gather(x, "row", axis=0, axis_index_groups=core_pairs)

    def over_row(x):
        return lax.all_to_all(x, "row", 0, 0, tiled=True, axis_index_groups=same_core)

    def over_col(x):
        return lax.all_to_all(x, "col", 0, 0, tiled=True)

    factor_cols = lax.dynamic_slice_in_dim(inv_factor, col_index * diag_width, diag_width, 1)
    factor_gram = lax.optimization_barrier(
        lax.dot_general(
            factor_cols,
            inv_factor,
            (((0,), (0,)), ((), ())),
            precision=lax.Precision.HIGHEST,
            preferred_element_type=F32,
        )
    )

    by_panel = pl.pallas_call(
        lambda *refs: scale_kernel(panel_blocks, *refs),
        out_shape=jax.ShapeDtypeStruct((row_count, chunk_rows, half + TAG), BF16),
        in_specs=[SMEM, VMEM, VMEM, VMEM],
        out_specs=VMEM,
        scratch_shapes=[pltpu.VMEM((slot_count * chunk_rows, width), F32)],
        compiler_params=FETCHING,
    )(
        slot_blocks,
        front_rows.reshape(slot_count * chunk_rows, width),
        inv_factor,
        jnp.asarray(order, BF16),
    )
    piece = pl.pallas_call(
        place_kernel,
        out_shape=jax.ShapeDtypeStruct((panel_blocks, chunk_rows, half), BF16),
        in_specs=[VMEM],
        out_specs=VMEM,
        compiler_params=PARAMS,
    )(lax.all_to_all(by_panel, "row", 0, 0, tiled=True))

    route = [
        ((2 * p + k) * col_count + c, (2 * int(table[p, c]) + k) * col_count + p)
        for p in range(col_count)
        for k in range(2)
        for c in range(col_count)
    ]
    turned = lax.ppermute(piece, ("row", "col"), route)
    parts = pair_gather(over_row(jnp.broadcast_to(turned[None], (chip_count, *turned.shape))))

    sent = pl.pallas_call(
        product_kernel,
        out_shape=jax.ShapeDtypeStruct((col_count, share + chunk_rows, width), BF16),
        in_specs=[SMEM, SMEM, VMEM, VMEM, VMEM, VMEM],
        out_specs=VMEM,
        scratch_shapes=[
            pltpu.VMEM((panel_rows, width), F32),
            pltpu.VMEM((col_count, share + chunk_rows, width), F32),
        ],
        compiler_params=PARAMS,
    )(col_arg, chip_arg, ancestor_inv, parts, piece, jnp.asarray(order.T, BF16))
    column_total, pair_factor = pl.pallas_call(
        total_kernel,
        out_shape=(
            jax.ShapeDtypeStruct((share, width), F32),
            jax.ShapeDtypeStruct((2 * share, half), F32),
        ),
        in_specs=[SMEM, VMEM],
        out_specs=(VMEM, VMEM),
        compiler_params=PARAMS,
    )(col_arg, over_col(sent))

    gram_half = lax.dot_general(
        pair_factor,
        pair_gather(column_total).reshape(2 * share, width),
        (((0,), (0,)), ((), ())),
        precision=lax.Precision.HIGH,
        preferred_element_type=F32,
    ).astype(BF16)
    copies = pl.pallas_call(
        copies_kernel,
        out_shape=jax.ShapeDtypeStruct((chip_count, diag_width // 2, width), BF16),
        in_specs=[VMEM],
        out_specs=VMEM,
        compiler_params=PARAMS,
    )(over_col(gram_half.reshape(col_count, diag_width // 2, width)))
    gram_rows = jnp.sum(over_row(copies).astype(F32), axis=0)
    gram_block = pair_gather(gram_rows).reshape(diag_width, width)
    return (-column_total, factor_gram + gram_block)


def solution(mesh):
    in_specs = (P("row", "col", None), P("row"), P(), P("row", "col"))
    out_specs = (P(("row", "col"), None), P("col", None))
    return jax.shard_map(body, mesh=mesh, in_specs=in_specs, out_specs=out_specs, check_vma=False)
```

```python
import itertools

import jax
import jax.numpy as jnp
import numpy as np
from jax import lax
from jax.experimental import pallas as pl
from jax.experimental.pallas import tpu as pltpu
from jax.sharding import PartitionSpec as P

BF16 = jnp.bfloat16
F32 = jnp.float32
TAG = 128
SMEM = pl.BlockSpec(memory_space=pltpu.SMEM)
VMEM = pl.BlockSpec(memory_space=pltpu.VMEM)
PARAMS = pltpu.CompilerParams(vmem_limit_bytes=16 * 2**20)
FETCHING = pltpu.CompilerParams(vmem_limit_bytes=60 * 2**20)


def dot(a, b, dims=((1,), (0,))):
    return lax.dot_general(a, b, (dims, ((), ())), preferred_element_type=F32)


def split(x):
    high = x.astype(BF16)
    return high, (x - high.astype(F32)).astype(BF16)


def by_core(width, group):
    part = group // 2
    column = np.arange(width)
    target = (column % group) // part * (width // 2) + column // group * part + column % part
    matrix = np.zeros((width, width), np.float32)
    matrix[column, target] = 1.0
    return matrix


def chip_position(chip, col, chip_count):
    ys = chip_count // 2
    return chip // ys * 2 + col % 2, chip % ys, col // 2


def hops(a, b, sizes):
    return sum(min((p - q) % n, (q - p) % n) for p, q, n in zip(a, b, sizes))


def short_routes(chip_count, col_count):
    sizes = (4, chip_count // 2, col_count // 2)
    table = np.zeros((col_count, col_count), np.int32)
    for p in range(col_count):
        source = [chip_position(p, c, chip_count) for c in range(col_count)]
        target = [chip_position(j, p, chip_count) for j in range(chip_count)]
        cost = [[hops(s, t, sizes) for t in target] for s in source]
        for limit in itertools.count():
            owner = {}

            def assign(c, seen):
                for j in range(chip_count):
                    if cost[c][j] <= limit and j not in seen:
                        seen.add(j)
                        if j not in owner or assign(owner[j], seen):
                            owner[j] = c
                            return True
                return False

            if all(assign(c, set()) for c in range(col_count)):
                break
        for j, c in owner.items():
            table[p, c] = j
    return table


def scale_kernel(panel_blocks, slots_ref, rows_ref, factor_ref, order_ref, out_ref, scaled_ref):
    half = factor_ref.shape[1] // 2
    high, low = split(factor_ref[...])
    rows = rows_ref[...]
    scaled = (dot(rows, high) + dot(rows, low)).astype(BF16)
    scaled_ref[...] = dot(scaled, order_ref[...])
    out_ref[...] = jnp.zeros_like(out_ref)
    slot_count = slots_ref.shape[0]
    height = rows_ref.shape[0] // slot_count
    for s in range(slot_count):
        block = slots_ref[s]

        @pl.when(block >= 0)
        def _():
            panel = block // panel_blocks
            number = (block - panel * panel_blocks + 1).astype(F32)
            for k in range(2):
                part = scaled_ref[s * height : (s + 1) * height, k * half : (k + 1) * half]
                out_ref[2 * panel + k, :, :half] = part.astype(BF16)
                out_ref[2 * panel + k, :, half:] = jnp.full((height, TAG), number, F32).astype(BF16)


def place_kernel(taken_ref, out_ref):
    width = taken_ref.shape[2] - TAG
    sources = range(taken_ref.shape[0])
    for lanes in range(0, width, TAG):
        totals = [jnp.zeros((taken_ref.shape[1], TAG), F32) for _ in range(out_ref.shape[0])]
        for s in sources:
            tag = taken_ref[s, :, width:].astype(F32)
            value = taken_ref[s, :, lanes : lanes + TAG].astype(F32)
            totals = [t + jnp.where(tag == n + 1, value, 0.0) for n, t in enumerate(totals)]
        for n, total in enumerate(totals):
            out_ref[n, :, lanes : lanes + TAG] = total.astype(BF16)


def product_kernel(chip_ref, tile_ref, parts_ref, back_ref, out_ref, panel_ref):
    chunks, blocks, height, half = parts_ref.shape[1:]
    for c in range(chunks):
        for b in range(blocks):
            first = (b * chunks + c) * height
            for k in range(2):
                rows = parts_ref[k, chip_ref[c], b].astype(F32)
                panel_ref[first : first + height, k * half : (k + 1) * half] = rows
    panel = dot(panel_ref[...].astype(BF16), back_ref[...]).astype(BF16)
    high, low = split(tile_ref[...])
    out_ref[...] = (dot(high, panel) + dot(low, panel)).astype(BF16)


def total_kernel(arrived_ref, total_ref, copies_ref):
    total = arrived_ref[0].astype(F32)
    for s in range(1, arrived_ref.shape[0]):
        total = total + arrived_ref[s].astype(F32)
    first = copies_ref.shape[1]
    rows = total[:first].astype(BF16)
    for copy in range(copies_ref.shape[0]):
        copies_ref[copy] = rows
    total_ref[...] = total[first:]


def body(front_rows, slot_blocks, inv_factor, ancestor_inv):
    col_count = lax.axis_size("col")
    row_count = lax.axis_size("row")
    chip_count = row_count // 2
    col_index = lax.axis_index("col")
    slot_count, chunk_rows, width = front_rows.shape
    half = width // 2
    tile_rows, panel_rows = ancestor_inv.shape
    block_rows = chunk_rows * col_count
    panel_blocks = panel_rows // block_rows
    share = tile_rows // col_count
    diag_width = width // col_count
    same_core = [[2 * j + k for j in range(chip_count)] for k in range(2)]
    core_pairs = [[2 * j, 2 * j + 1] for j in range(chip_count)]
    order = by_core(width, diag_width)
    table = short_routes(chip_count, col_count)
    chip_arg = lax.dynamic_index_in_dim(jnp.asarray(table), col_index, 0, keepdims=False)

    def pair_gather(x):
        return lax.all_gather(x, "row", axis=0, axis_index_groups=core_pairs)

    def over_row(x):
        return lax.all_to_all(x, "row", 0, 0, tiled=True, axis_index_groups=same_core)

    def over_col(x):
        return lax.all_to_all(x, "col", 0, 0, tiled=True)

    factor_cols = lax.dynamic_slice_in_dim(inv_factor, col_index * diag_width, diag_width, 1)
    factor_gram = lax.optimization_barrier(
        lax.dot_general(
            factor_cols,
            inv_factor,
            (((0,), (0,)), ((), ())),
            precision=lax.Precision.HIGHEST,
            preferred_element_type=F32,
        )
    )

    by_panel = pl.pallas_call(
        lambda *refs: scale_kernel(panel_blocks, *refs),
        out_shape=jax.ShapeDtypeStruct((row_count, chunk_rows, half + TAG), BF16),
        in_specs=[SMEM, VMEM, VMEM, VMEM],
        out_specs=VMEM,
        scratch_shapes=[pltpu.VMEM((slot_count * chunk_rows, width), F32)],
        compiler_params=FETCHING,
    )(
        slot_blocks,
        front_rows.reshape(slot_count * chunk_rows, width),
        inv_factor,
        jnp.asarray(order, BF16),
    )
    piece = pl.pallas_call(
        place_kernel,
        out_shape=jax.ShapeDtypeStruct((panel_blocks, chunk_rows, half), BF16),
        in_specs=[VMEM],
        out_specs=VMEM,
        compiler_params=PARAMS,
    )(lax.all_to_all(by_panel, "row", 0, 0, tiled=True))

    route = [
        ((2 * p + k) * col_count + c, (2 * int(table[p, c]) + k) * col_count + p)
        for p in range(col_count)
        for k in range(2)
        for c in range(col_count)
    ]
    turned = lax.ppermute(piece, ("row", "col"), route)
    pair_factor = over_col(jnp.broadcast_to(piece[None], (col_count, *piece.shape)))
    pair_factor = pair_factor.transpose(1, 0, 2, 3).reshape(2 * tile_rows, half)
    parts = pair_gather(over_row(jnp.broadcast_to(turned[None], (chip_count, *turned.shape))))

    partial_sums = pl.pallas_call(
        product_kernel,
        out_shape=jax.ShapeDtypeStruct((tile_rows, width), BF16),
        in_specs=[SMEM, VMEM, VMEM, VMEM],
        out_specs=VMEM,
        scratch_shapes=[pltpu.VMEM((panel_rows, width), F32)],
        compiler_params=PARAMS,
    )(chip_arg, ancestor_inv, parts, jnp.asarray(order.T, BF16))
    pair_sums = pair_gather(partial_sums).reshape(2 * tile_rows, width)
    gram_half = dot(pair_factor, pair_sums, ((0,), (0,))).astype(BF16)
    sent = jnp.concatenate(
        [
            gram_half.reshape(col_count, diag_width // 2, width),
            partial_sums.reshape(col_count, share, width),
        ],
        1,
    )
    column_total, copies = pl.pallas_call(
        total_kernel,
        out_shape=(
            jax.ShapeDtypeStruct((share, width), F32),
            jax.ShapeDtypeStruct((chip_count, diag_width // 2, width), BF16),
        ),
        in_specs=[VMEM],
        out_specs=(VMEM, VMEM),
        compiler_params=PARAMS,
    )(over_col(sent))
    gram_rows = jnp.sum(over_row(copies).astype(F32), axis=0)
    gram_block = pair_gather(gram_rows).reshape(diag_width, width)
    return (-column_total, factor_gram + gram_block)


def solution(mesh):
    in_specs = (P("row", "col", None), P("row"), P(), P("row", "col"))
    out_specs = (P(("row", "col"), None), P("col", None))
    return jax.shard_map(body, mesh=mesh, in_specs=in_specs, out_specs=out_specs, check_vma=False)
```

```python
import itertools

import jax
import jax.numpy as jnp
import numpy as np
from jax import lax
from jax.experimental import pallas as pl
from jax.experimental.pallas import tpu as pltpu
from jax.sharding import PartitionSpec as P

BF16 = jnp.bfloat16
F32 = jnp.float32
TAG = 128
SMEM = pl.BlockSpec(memory_space=pltpu.SMEM)
VMEM = pl.BlockSpec(memory_space=pltpu.VMEM)
PARAMS = pltpu.CompilerParams(vmem_limit_bytes=16 * 2**20)
FETCHING = pltpu.CompilerParams(vmem_limit_bytes=60 * 2**20)


def dot(a, b, dims=((1,), (0,))):
    return lax.dot_general(a, b, (dims, ((), ())), preferred_element_type=F32)


def split(x):
    high = x.astype(BF16)
    return high, (x - high.astype(F32)).astype(BF16)


def chip_position(chip, col, chip_count):
    ys = chip_count // 2
    return chip // ys * 2 + col % 2, chip % ys, col // 2


def hops(a, b, sizes):
    return sum(min((p - q) % n, (q - p) % n) for p, q, n in zip(a, b, sizes))


def short_routes(chip_count, col_count):
    sizes = (4, chip_count // 2, col_count // 2)
    table = np.zeros((col_count, col_count), np.int32)
    for p in range(col_count):
        source = [chip_position(p, c, chip_count) for c in range(col_count)]
        target = [chip_position(j, p, chip_count) for j in range(chip_count)]
        cost = [[hops(s, t, sizes) for t in target] for s in source]
        for limit in itertools.count():
            owner = {}

            def assign(c, seen):
                for j in range(chip_count):
                    if cost[c][j] <= limit and j not in seen:
                        seen.add(j)
                        if j not in owner or assign(owner[j], seen):
                            owner[j] = c
                            return True
                return False

            if all(assign(c, set()) for c in range(col_count)):
                break
        for j, c in owner.items():
            table[p, c] = j
    return table


def scale_kernel(panel_blocks, slots_ref, rows_ref, factor_ref, out_ref, scaled_ref):
    half = factor_ref.shape[1] // 2
    high, low = split(factor_ref[...])
    rows = rows_ref[...]
    scaled_ref[...] = dot(rows, high) + dot(rows, low)
    out_ref[...] = jnp.zeros_like(out_ref)
    slot_count = slots_ref.shape[0]
    height = rows_ref.shape[0] // slot_count
    for s in range(slot_count):
        block = slots_ref[s]

        @pl.when(block >= 0)
        def _():
            panel = block // panel_blocks
            number = (block - panel * panel_blocks + 1).astype(F32)
            for k in range(2):
                part = scaled_ref[s * height : (s + 1) * height, k * half : (k + 1) * half]
                out_ref[2 * panel + k, :, :half] = part.astype(BF16)
                out_ref[2 * panel + k, :, half:] = jnp.full((height, TAG), number, F32).astype(BF16)


def place_kernel(taken_ref, out_ref):
    width = taken_ref.shape[2] - TAG
    sources = range(taken_ref.shape[0])
    for lanes in range(0, width, TAG):
        totals = [jnp.zeros((taken_ref.shape[1], TAG), F32) for _ in range(out_ref.shape[0])]
        for s in sources:
            tag = taken_ref[s, :, width:].astype(F32)
            value = taken_ref[s, :, lanes : lanes + TAG].astype(F32)
            totals = [t + jnp.where(tag == n + 1, value, 0.0) for n, t in enumerate(totals)]
        for n, total in enumerate(totals):
            out_ref[n, :, lanes : lanes + TAG] = total.astype(BF16)


def product_kernel(core_ref, chip_ref, own_ref, other_ref, parts_ref, factor_ref, out_ref, panel_ref, sums_ref, sent_ref):
    chunks, blocks, height, half = parts_ref.shape
    for c in range(chunks):
        for b in range(blocks):
            first = (b * chunks + c) * height
            panel_ref[first : first + height, :] = parts_ref[chip_ref[c], b].astype(F32)
    panel = panel_ref[...].astype(BF16)
    tile_rows = own_ref.shape[0]
    for k, ref in ((core_ref[0], own_ref), (1 - core_ref[0], other_ref)):
        high, low = split(ref[...])
        at = pl.ds(pl.multiple_of(k * tile_rows, tile_rows), tile_rows)
        sums_ref[at, :] = dot(high, panel) + dot(low, panel)
    sums = sums_ref[...]
    gram = dot(factor_ref[...], sums.astype(BF16))
    rows = gram.shape[0] // chunks
    share = sums.shape[0] // 2 // chunks
    sent_ref[:, :rows, :] = gram.reshape(chunks, rows, half)
    sums = sums.reshape(2, chunks, share, half)
    for k in range(2):
        sent_ref[:, rows + k * share : rows + (k + 1) * share, :] = sums[k]
    out_ref[...] = sent_ref[...].astype(BF16)


def total_kernel(arrived_ref, total_ref, copies_ref):
    total = arrived_ref[0].astype(F32)
    for s in range(1, arrived_ref.shape[0]):
        total = total + arrived_ref[s].astype(F32)
    first = copies_ref.shape[1]
    rows = total[:first].astype(BF16)
    for copy in range(copies_ref.shape[0]):
        copies_ref[copy] = rows
    total_ref[...] = total[first:]


def body(front_rows, slot_blocks, inv_factor, ancestor_inv):
    col_count = lax.axis_size("col")
    row_count = lax.axis_size("row")
    chip_count = row_count // 2
    col_index = lax.axis_index("col")
    core = lax.axis_index("row") % 2
    core_arg = jnp.reshape(core, (1,)).astype(jnp.int32)
    slot_count, chunk_rows, width = front_rows.shape
    half = width // 2
    tile_rows, panel_rows = ancestor_inv.shape
    block_rows = chunk_rows * col_count
    panel_blocks = panel_rows // block_rows
    share = tile_rows // col_count
    diag_width = width // col_count
    same_core = [[2 * j + k for j in range(chip_count)] for k in range(2)]
    core_swap = [(i, i ^ 1) for i in range(row_count)]
    core_pairs = [[2 * j, 2 * j + 1] for j in range(chip_count)]
    table = short_routes(chip_count, col_count)
    chip_arg = lax.dynamic_index_in_dim(jnp.asarray(table), col_index, 0, keepdims=False)

    def pair_gather(x):
        return lax.all_gather(x, "row", axis=0, axis_index_groups=core_pairs)

    def over_row(x):
        return lax.all_to_all(x, "row", 0, 0, tiled=True, axis_index_groups=same_core)

    def over_col(x):
        return lax.all_to_all(x, "col", 0, 0, tiled=True)

    factor_cols = lax.dynamic_slice_in_dim(inv_factor, col_index * diag_width, diag_width, 1)
    factor_gram = lax.optimization_barrier(
        lax.dot_general(
            factor_cols,
            inv_factor,
            (((0,), (0,)), ((), ())),
            precision=lax.Precision.HIGHEST,
            preferred_element_type=F32,
        )
    )

    by_panel = pl.pallas_call(
        lambda *refs: scale_kernel(panel_blocks, *refs),
        out_shape=jax.ShapeDtypeStruct((row_count, chunk_rows, half + TAG), BF16),
        in_specs=[SMEM, VMEM, VMEM],
        out_specs=VMEM,
        scratch_shapes=[pltpu.VMEM((slot_count * chunk_rows, width), F32)],
        compiler_params=FETCHING,
    )(
        slot_blocks,
        front_rows.reshape(slot_count * chunk_rows, width),
        inv_factor,
    )
    taken = lax.all_to_all(by_panel, "row", 0, 0, tiled=True)
    piece = pl.pallas_call(
        place_kernel,
        out_shape=jax.ShapeDtypeStruct((panel_blocks, chunk_rows, half), BF16),
        in_specs=[VMEM],
        out_specs=VMEM,
        compiler_params=PARAMS,
    )(taken)

    route = [
        ((2 * p + k) * col_count + c, (2 * int(table[p, c]) + k) * col_count + p)
        for p in range(col_count)
        for k in range(2)
        for c in range(col_count)
    ]
    turned = lax.ppermute(piece, ("row", "col"), route)
    turned, own_tile = lax.optimization_barrier((turned, ancestor_inv))
    other_tile = lax.ppermute(own_tile, "row", core_swap)
    factor = over_col(jnp.broadcast_to(piece[None], (col_count, *piece.shape)))
    tile_factor = pair_gather(factor)
    tile_factor = tile_factor.transpose(0, 4, 2, 1, 3).reshape(width, 2 * tile_rows)
    parts = over_row(jnp.broadcast_to(turned[None], (chip_count, *turned.shape)))

    sent = (col_count, diag_width + 2 * share, half)
    sent = pl.pallas_call(
        product_kernel,
        out_shape=jax.ShapeDtypeStruct(sent, BF16),
        in_specs=[SMEM, SMEM, VMEM, VMEM, VMEM, VMEM],
        out_specs=VMEM,
        scratch_shapes=[
            pltpu.VMEM((panel_rows, half), F32),
            pltpu.VMEM((2 * tile_rows, half), F32),
            pltpu.VMEM(sent, F32),
        ],
        compiler_params=PARAMS,
    )(core_arg, chip_arg, ancestor_inv, other_tile, parts, tile_factor)
    totals, copies = pl.pallas_call(
        total_kernel,
        out_shape=(
            jax.ShapeDtypeStruct((2 * share, half), F32),
            jax.ShapeDtypeStruct((chip_count, diag_width, half), BF16),
        ),
        in_specs=[VMEM],
        out_specs=(VMEM, VMEM),
        compiler_params=PARAMS,
    )(over_col(sent))
    halves = pair_gather(totals).reshape(2, 2, share, half)
    product = lax.dynamic_index_in_dim(halves, core, 1, keepdims=False)
    product = jnp.concatenate([product[0], product[1]], 1)
    gram_rows = pair_gather(jnp.sum(over_row(copies).astype(F32), axis=0))
    gram_rows = jnp.concatenate([gram_rows[0], gram_rows[1]], 1)
    return (-product, factor_gram + gram_rows)


def solution(mesh):
    in_specs = (P("row", "col", None), P("row"), P(), P("row", "col"))
    out_specs = (P(("row", "col"), None), P("col", None))
    return jax.shard_map(body, mesh=mesh, in_specs=in_specs, out_specs=out_specs, check_vma=False)
```

```python
import itertools

import jax
import jax.numpy as jnp
import numpy as np
from jax import lax
from jax.experimental import pallas as pl
from jax.experimental.pallas import tpu as pltpu
from jax.sharding import PartitionSpec as P

BF16 = jnp.bfloat16
F32 = jnp.float32
TAG = 128
SMEM = pl.BlockSpec(memory_space=pltpu.SMEM)
VMEM = pl.BlockSpec(memory_space=pltpu.VMEM)
PARAMS = pltpu.CompilerParams(vmem_limit_bytes=16 * 2**20)
FETCHING = pltpu.CompilerParams(vmem_limit_bytes=60 * 2**20)


def dot(a, b, dims=((1,), (0,))):
    return lax.dot_general(a, b, (dims, ((), ())), preferred_element_type=F32)


def split(x):
    high = x.astype(BF16)
    return high, (x - high.astype(F32)).astype(BF16)


def chip_position(chip, col, chip_count):
    ys = chip_count // 2
    return chip // ys * 2 + col % 2, chip % ys, col // 2


def hops(a, b, sizes):
    return sum(min((p - q) % n, (q - p) % n) for p, q, n in zip(a, b, sizes))


def short_routes(chip_count, col_count):
    sizes = (4, chip_count // 2, col_count // 2)
    table = np.zeros((col_count, col_count), np.int32)
    for p in range(col_count):
        source = [chip_position(p, c, chip_count) for c in range(col_count)]
        target = [chip_position(j, p, chip_count) for j in range(chip_count)]
        cost = [[hops(s, t, sizes) for t in target] for s in source]
        for limit in itertools.count():
            owner = {}

            def assign(c, seen):
                for j in range(chip_count):
                    if cost[c][j] <= limit and j not in seen:
                        seen.add(j)
                        if j not in owner or assign(owner[j], seen):
                            owner[j] = c
                            return True
                return False

            if all(assign(c, set()) for c in range(col_count)):
                break
        for j, c in owner.items():
            table[p, c] = j
    return table


def scale_kernel(panel_blocks, slots_ref, rows_ref, factor_ref, out_ref, scaled_ref):
    half = factor_ref.shape[1] // 2
    high, low = split(factor_ref[...])
    rows = rows_ref[...]
    scaled_ref[...] = dot(rows, high) + dot(rows, low)
    out_ref[...] = jnp.zeros_like(out_ref)
    slot_count = slots_ref.shape[0]
    height = rows_ref.shape[0] // slot_count
    for s in range(slot_count):
        block = slots_ref[s]

        @pl.when(block >= 0)
        def _():
            panel = block // panel_blocks
            number = (block - panel * panel_blocks + 1).astype(F32)
            for k in range(2):
                part = scaled_ref[s * height : (s + 1) * height, k * half : (k + 1) * half]
                out_ref[2 * panel + k, :, :half] = part.astype(BF16)
                out_ref[2 * panel + k, :, half:] = jnp.full((height, TAG), number, F32).astype(BF16)


def place_kernel(taken_ref, out_ref):
    width = taken_ref.shape[2] - TAG
    sources = range(taken_ref.shape[0])
    for lanes in range(0, width, TAG):
        totals = [jnp.zeros((taken_ref.shape[1], TAG), F32) for _ in range(out_ref.shape[0])]
        for s in sources:
            tag = taken_ref[s, :, width:].astype(F32)
            value = taken_ref[s, :, lanes : lanes + TAG].astype(F32)
            totals = [t + jnp.where(tag == n + 1, value, 0.0) for n, t in enumerate(totals)]
        for n, total in enumerate(totals):
            out_ref[n, :, lanes : lanes + TAG] = total.astype(BF16)


def product_kernel(chip_ref, tiles_ref, parts_ref, factor_ref, out_ref, panel_ref, sent_ref):
    chunks, blocks, height, half = parts_ref.shape
    for c in range(chunks):
        for b in range(blocks):
            first = (b * chunks + c) * height
            panel_ref[first : first + height, :] = parts_ref[chip_ref[c], b].astype(F32)
    panel = panel_ref[...].astype(BF16)
    high, low = split(tiles_ref[...])
    sums = dot(high, panel) + dot(low, panel)
    gram = dot(factor_ref[...], sums.astype(BF16))
    rows = gram.shape[0] // chunks
    share = sums.shape[0] // 2 // chunks
    sent_ref[:, :rows, :] = gram.reshape(chunks, rows, half)
    sums = sums.reshape(2, chunks, share, half)
    for k in range(2):
        sent_ref[:, rows + k * share : rows + (k + 1) * share, :] = sums[k]
    out_ref[...] = sent_ref[...].astype(BF16)


def total_kernel(arrived_ref, total_ref, copies_ref):
    total = arrived_ref[0].astype(F32)
    for s in range(1, arrived_ref.shape[0]):
        total = total + arrived_ref[s].astype(F32)
    first = copies_ref.shape[1]
    rows = total[:first].astype(BF16)
    for copy in range(copies_ref.shape[0]):
        copies_ref[copy] = rows
    total_ref[...] = total[first:]


def body(front_rows, slot_blocks, inv_factor, ancestor_inv):
    col_count = lax.axis_size("col")
    row_count = lax.axis_size("row")
    chip_count = row_count // 2
    col_index = lax.axis_index("col")
    core = lax.axis_index("row") % 2
    slot_count, chunk_rows, width = front_rows.shape
    half = width // 2
    tile_rows, panel_rows = ancestor_inv.shape
    block_rows = chunk_rows * col_count
    panel_blocks = panel_rows // block_rows
    share = tile_rows // col_count
    diag_width = width // col_count
    same_core = [[2 * j + k for j in range(chip_count)] for k in range(2)]
    core_pairs = [[2 * j, 2 * j + 1] for j in range(chip_count)]
    table = short_routes(chip_count, col_count)
    chip_arg = lax.dynamic_index_in_dim(jnp.asarray(table), col_index, 0, keepdims=False)

    def pair_gather(x):
        return lax.all_gather(x, "row", axis=0, axis_index_groups=core_pairs)

    def over_row(x):
        return lax.all_to_all(x, "row", 0, 0, tiled=True, axis_index_groups=same_core)

    def over_col(x):
        return lax.all_to_all(x, "col", 0, 0, tiled=True)

    factor_cols = lax.dynamic_slice_in_dim(inv_factor, col_index * diag_width, diag_width, 1)
    factor_gram = lax.optimization_barrier(
        lax.dot_general(
            factor_cols,
            inv_factor,
            (((0,), (0,)), ((), ())),
            precision=lax.Precision.HIGHEST,
            preferred_element_type=F32,
        )
    )

    tiles = pair_gather(ancestor_inv).reshape(2 * tile_rows, panel_rows)

    by_panel = pl.pallas_call(
        lambda *refs: scale_kernel(panel_blocks, *refs),
        out_shape=jax.ShapeDtypeStruct((row_count, chunk_rows, half + TAG), BF16),
        in_specs=[SMEM, VMEM, VMEM],
        out_specs=VMEM,
        scratch_shapes=[pltpu.VMEM((slot_count * chunk_rows, width), F32)],
        compiler_params=FETCHING,
    )(
        slot_blocks,
        front_rows.reshape(slot_count * chunk_rows, width),
        inv_factor,
    )
    taken = lax.all_to_all(by_panel, "row", 0, 0, tiled=True)
    piece = pl.pallas_call(
        place_kernel,
        out_shape=jax.ShapeDtypeStruct((panel_blocks, chunk_rows, half), BF16),
        in_specs=[VMEM],
        out_specs=VMEM,
        compiler_params=PARAMS,
    )(taken)

    route = [
        ((2 * p + k) * col_count + c, (2 * int(table[p, c]) + k) * col_count + p)
        for p in range(col_count)
        for k in range(2)
        for c in range(col_count)
    ]
    turned = lax.ppermute(piece, ("row", "col"), route)
    factor = over_col(jnp.broadcast_to(piece[None], (col_count, *piece.shape)))
    tile_factor, tiles = lax.optimization_barrier((pair_gather(factor), tiles))
    tile_factor = tile_factor.transpose(0, 4, 2, 1, 3).reshape(width, 2 * tile_rows)
    parts = over_row(jnp.broadcast_to(turned[None], (chip_count, *turned.shape)))

    sent = (col_count, diag_width + 2 * share, half)
    sent = pl.pallas_call(
        product_kernel,
        out_shape=jax.ShapeDtypeStruct(sent, BF16),
        in_specs=[SMEM, VMEM, VMEM, VMEM],
        out_specs=VMEM,
        scratch_shapes=[
            pltpu.VMEM((panel_rows, half), F32),
            pltpu.VMEM(sent, F32),
        ],
        compiler_params=PARAMS,
    )(chip_arg, tiles, parts, tile_factor)
    totals, copies = pl.pallas_call(
        total_kernel,
        out_shape=(
            jax.ShapeDtypeStruct((2 * share, half), F32),
            jax.ShapeDtypeStruct((chip_count, diag_width, half), BF16),
        ),
        in_specs=[VMEM],
        out_specs=(VMEM, VMEM),
        compiler_params=PARAMS,
    )(over_col(sent))
    halves = pair_gather(totals).reshape(2, 2, share, half)
    product = lax.dynamic_index_in_dim(halves, core, 1, keepdims=False)
    product = jnp.concatenate([product[0], product[1]], 1)
    gram_rows = pair_gather(jnp.sum(over_row(copies).astype(F32), axis=0))
    gram_rows = jnp.concatenate([gram_rows[0], gram_rows[1]], 1)
    return (-product, factor_gram + gram_rows)


def solution(mesh):
    in_specs = (P("row", "col", None), P("row"), P(), P("row", "col"))
    out_specs = (P(("row", "col"), None), P("col", None))
    return jax.shard_map(body, mesh=mesh, in_specs=in_specs, out_specs=out_specs, check_vma=False)
```

```python
import itertools

import jax
import jax.numpy as jnp
import numpy as np
from jax import lax
from jax.experimental import pallas as pl
from jax.experimental.pallas import tpu as pltpu
from jax.sharding import PartitionSpec as P

BF16 = jnp.bfloat16
F32 = jnp.float32
TAG = 128
SMEM = pl.BlockSpec(memory_space=pltpu.SMEM)
VMEM = pl.BlockSpec(memory_space=pltpu.VMEM)
PARAMS = pltpu.CompilerParams(vmem_limit_bytes=16 * 2**20)
FETCHING = pltpu.CompilerParams(vmem_limit_bytes=60 * 2**20)


def dot(a, b, dims=((1,), (0,))):
    return lax.dot_general(a, b, (dims, ((), ())), preferred_element_type=F32)


def split(x):
    high = x.astype(BF16)
    return high, (x - high.astype(F32)).astype(BF16)


def chip_position(chip, col, chip_count):
    ys = chip_count // 2
    return chip // ys * 2 + col % 2, chip % ys, col // 2


def hops(a, b, sizes):
    return sum(min((p - q) % n, (q - p) % n) for p, q, n in zip(a, b, sizes))


def short_routes(chip_count, col_count):
    sizes = (4, chip_count // 2, col_count // 2)
    table = np.zeros((col_count, col_count), np.int32)
    for p in range(col_count):
        source = [chip_position(p, c, chip_count) for c in range(col_count)]
        target = [chip_position(j, p, chip_count) for j in range(chip_count)]
        cost = [[hops(s, t, sizes) for t in target] for s in source]
        for limit in itertools.count():
            owner = {}

            def assign(c, seen):
                for j in range(chip_count):
                    if cost[c][j] <= limit and j not in seen:
                        seen.add(j)
                        if j not in owner or assign(owner[j], seen):
                            owner[j] = c
                            return True
                return False

            if all(assign(c, set()) for c in range(col_count)):
                break
        for j, c in owner.items():
            table[p, c] = j
    return table


def scale_kernel(panel_blocks, slots_ref, rows_ref, factor_ref, out_ref, scaled_ref):
    half = factor_ref.shape[1] // 2
    high, low = split(factor_ref[...])
    rows = rows_ref[...]
    scaled_ref[...] = dot(rows, high) + dot(rows, low)
    out_ref[...] = jnp.zeros_like(out_ref)
    slot_count = slots_ref.shape[0]
    height = rows_ref.shape[0] // slot_count
    for s in range(slot_count):
        block = slots_ref[s]

        @pl.when(block >= 0)
        def _():
            panel = block // panel_blocks
            number = (block - panel * panel_blocks + 1).astype(F32)
            for k in range(2):
                part = scaled_ref[s * height : (s + 1) * height, k * half : (k + 1) * half]
                out_ref[2 * panel + k, :, :half] = part.astype(BF16)
                out_ref[2 * panel + k, :, half:] = jnp.full((height, TAG), number, F32).astype(BF16)


def place_kernel(taken_ref, out_ref):
    width = taken_ref.shape[2] - TAG
    sources = range(taken_ref.shape[0])
    for lanes in range(0, width, TAG):
        totals = [jnp.zeros((taken_ref.shape[1], TAG), F32) for _ in range(out_ref.shape[0])]
        for s in sources:
            tag = taken_ref[s, :, width:].astype(F32)
            value = taken_ref[s, :, lanes : lanes + TAG].astype(F32)
            totals = [t + jnp.where(tag == n + 1, value, 0.0) for n, t in enumerate(totals)]
        for n, total in enumerate(totals):
            out_ref[n, :, lanes : lanes + TAG] = total.astype(BF16)


def product_kernel(chip_ref, *refs):
    *tile_refs, parts_ref, factor_ref, out_ref, panel_ref, high_ref, low_ref, sent_ref = refs
    chunks, blocks, height, half = parts_ref.shape
    for b, ref in enumerate(tile_refs):
        rows = ref.shape[1]
        for k in range(2):
            first = (k * len(tile_refs) + b) * rows
            high_ref[first : first + rows, :], low_ref[first : first + rows, :] = split(ref[k])
    for c in range(chunks):
        for b in range(blocks):
            first = (b * chunks + c) * height
            panel_ref[first : first + height, :] = parts_ref[chip_ref[c], b].astype(F32)
    panel = panel_ref[...].astype(BF16)
    sums = dot(high_ref[...], panel) + dot(low_ref[...], panel)
    gram = dot(factor_ref[...], sums.astype(BF16))
    rows = gram.shape[0] // chunks
    share = sums.shape[0] // 2 // chunks
    sent_ref[:, :rows, :] = gram.reshape(chunks, rows, half)
    sums = sums.reshape(2, chunks, share, half)
    for k in range(2):
        sent_ref[:, rows + k * share : rows + (k + 1) * share, :] = sums[k]
    out_ref[...] = sent_ref[...].astype(BF16)


def total_kernel(arrived_ref, total_ref, copies_ref):
    total = arrived_ref[0].astype(F32)
    for s in range(1, arrived_ref.shape[0]):
        total = total + arrived_ref[s].astype(F32)
    first = copies_ref.shape[1]
    rows = total[:first].astype(BF16)
    for copy in range(copies_ref.shape[0]):
        copies_ref[copy] = rows
    total_ref[...] = total[first:]


def body(front_rows, slot_blocks, inv_factor, ancestor_inv):
    col_count = lax.axis_size("col")
    row_count = lax.axis_size("row")
    chip_count = row_count // 2
    col_index = lax.axis_index("col")
    core = lax.axis_index("row") % 2
    slot_count, chunk_rows, width = front_rows.shape
    half = width // 2
    tile_rows, panel_rows = ancestor_inv.shape
    block_rows = chunk_rows * col_count
    panel_blocks = panel_rows // block_rows
    share = tile_rows // col_count
    diag_width = width // col_count
    same_core = [[2 * j + k for j in range(chip_count)] for k in range(2)]
    core_pairs = [[2 * j, 2 * j + 1] for j in range(chip_count)]
    table = short_routes(chip_count, col_count)
    chip_arg = lax.dynamic_index_in_dim(jnp.asarray(table), col_index, 0, keepdims=False)

    def pair_gather(x):
        return lax.all_gather(x, "row", axis=0, axis_index_groups=core_pairs)

    def over_row(x):
        return lax.all_to_all(x, "row", 0, 0, tiled=True, axis_index_groups=same_core)

    def over_col(x):
        return lax.all_to_all(x, "col", 0, 0, tiled=True)

    factor_cols = lax.dynamic_slice_in_dim(inv_factor, col_index * diag_width, diag_width, 1)
    factor_gram = lax.dot_general(
        factor_cols,
        inv_factor,
        (((0,), (0,)), ((), ())),
        precision=lax.Precision.HIGHEST,
        preferred_element_type=F32,
    )

    by_panel = pl.pallas_call(
        lambda *refs: scale_kernel(panel_blocks, *refs),
        out_shape=jax.ShapeDtypeStruct((row_count, chunk_rows, half + TAG), BF16),
        in_specs=[SMEM, VMEM, VMEM],
        out_specs=VMEM,
        scratch_shapes=[pltpu.VMEM((slot_count * chunk_rows, width), F32)],
        compiler_params=FETCHING,
    )(
        slot_blocks,
        front_rows.reshape(slot_count * chunk_rows, width),
        inv_factor,
    )
    by_panel, tile = lax.optimization_barrier((by_panel, ancestor_inv))
    tiles = [
        pair_gather(tile[first : first + block_rows]) for first in range(0, tile_rows, block_rows)
    ]
    taken, factor_gram, core, *tiles = lax.optimization_barrier(
        (lax.all_to_all(by_panel, "row", 0, 0, tiled=True), factor_gram, core, *tiles)
    )
    piece = pl.pallas_call(
        place_kernel,
        out_shape=jax.ShapeDtypeStruct((panel_blocks, chunk_rows, half), BF16),
        in_specs=[VMEM],
        out_specs=VMEM,
        compiler_params=PARAMS,
    )(taken)

    route = [
        ((2 * p + k) * col_count + c, (2 * int(table[p, c]) + k) * col_count + p)
        for p in range(col_count)
        for k in range(2)
        for c in range(col_count)
    ]
    turned = lax.ppermute(piece, ("row", "col"), route)
    factor = over_col(jnp.broadcast_to(piece[None], (col_count, *piece.shape)))
    tile_factor = pair_gather(factor)
    tile_factor = tile_factor.transpose(0, 4, 2, 1, 3).reshape(width, 2 * tile_rows)
    parts = over_row(jnp.broadcast_to(turned[None], (chip_count, *turned.shape)))

    sent = (col_count, diag_width + 2 * share, half)
    sent = pl.pallas_call(
        product_kernel,
        out_shape=jax.ShapeDtypeStruct(sent, BF16),
        in_specs=[SMEM] + [VMEM] * (len(tiles) + 2),
        out_specs=VMEM,
        scratch_shapes=[
            pltpu.VMEM((panel_rows, half), F32),
            pltpu.VMEM((2 * tile_rows, panel_rows), BF16),
            pltpu.VMEM((2 * tile_rows, panel_rows), BF16),
            pltpu.VMEM(sent, F32),
        ],
        compiler_params=pltpu.CompilerParams(vmem_limit_bytes=52 * 2**20),
    )(chip_arg, *tiles, parts, tile_factor)
    totals, copies = pl.pallas_call(
        total_kernel,
        out_shape=(
            jax.ShapeDtypeStruct((2 * share, half), F32),
            jax.ShapeDtypeStruct((chip_count, diag_width, half), BF16),
        ),
        in_specs=[VMEM],
        out_specs=(VMEM, VMEM),
        compiler_params=PARAMS,
    )(over_col(sent))
    halves = pair_gather(totals).reshape(2, 2, share, half)
    product = jnp.where(core == 0, halves[:, 0], halves[:, 1])
    product = jnp.concatenate([product[0], product[1]], 1)
    gram_rows = pair_gather(jnp.sum(over_row(copies).astype(F32), axis=0))
    gram_rows = jnp.concatenate([gram_rows[0], gram_rows[1]], 1)
    return (-product, factor_gram + gram_rows)


def solution(mesh):
    in_specs = (P("row", "col", None), P("row"), P(), P("row", "col"))
    out_specs = (P(("row", "col"), None), P("col", None))
    return jax.shard_map(body, mesh=mesh, in_specs=in_specs, out_specs=out_specs, check_vma=False)
```

```python
import itertools

import jax
import jax.numpy as jnp
import numpy as np
from jax import lax
from jax.experimental import pallas as pl
from jax.experimental.pallas import tpu as pltpu
from jax.sharding import PartitionSpec as P

BF16 = jnp.bfloat16
F32 = jnp.float32
TAG = 128
SMEM = pl.BlockSpec(memory_space=pltpu.SMEM)
VMEM = pl.BlockSpec(memory_space=pltpu.VMEM)
PARAMS = pltpu.CompilerParams(vmem_limit_bytes=16 * 2**20)
FETCHING = pltpu.CompilerParams(vmem_limit_bytes=60 * 2**20)


def dot(a, b, dims=((1,), (0,))):
    return lax.dot_general(a, b, (dims, ((), ())), preferred_element_type=F32)


def split(x):
    high = x.astype(BF16)
    return high, (x - high.astype(F32)).astype(BF16)


def chip_position(chip, col, chip_count):
    ys = chip_count // 2
    return chip // ys * 2 + col % 2, chip % ys, col // 2


def hops(a, b, sizes):
    return sum(min((p - q) % n, (q - p) % n) for p, q, n in zip(a, b, sizes))


def short_routes(chip_count, col_count):
    sizes = (4, chip_count // 2, col_count // 2)
    table = np.zeros((col_count, col_count), np.int32)
    for p in range(col_count):
        source = [chip_position(p, c, chip_count) for c in range(col_count)]
        target = [chip_position(j, p, chip_count) for j in range(chip_count)]
        cost = [[hops(s, t, sizes) for t in target] for s in source]
        for limit in itertools.count():
            owner = {}

            def assign(c, seen):
                for j in range(chip_count):
                    if cost[c][j] <= limit and j not in seen:
                        seen.add(j)
                        if j not in owner or assign(owner[j], seen):
                            owner[j] = c
                            return True
                return False

            if all(assign(c, set()) for c in range(col_count)):
                break
        for j, c in owner.items():
            table[p, c] = j
    return table


def scale_kernel(panel_blocks, slots_ref, rows_ref, factor_ref, out_ref, scaled_ref):
    half = factor_ref.shape[1] // 2
    high, low = split(factor_ref[...])
    rows = rows_ref[...]
    scaled_ref[...] = dot(rows, high) + dot(rows, low)
    out_ref[...] = jnp.zeros_like(out_ref)
    slot_count = slots_ref.shape[0]
    height = rows_ref.shape[0] // slot_count
    for s in range(slot_count):
        block = slots_ref[s]

        @pl.when(block >= 0)
        def _():
            panel = block // panel_blocks
            number = (block - panel * panel_blocks + 1).astype(F32)
            for k in range(2):
                part = scaled_ref[s * height : (s + 1) * height, k * half : (k + 1) * half]
                out_ref[2 * panel + k, :, :half] = part.astype(BF16)
                out_ref[2 * panel + k, :, half:] = jnp.full((height, TAG), number, F32).astype(BF16)


def place_kernel(taken_ref, out_ref):
    width = taken_ref.shape[2] - TAG
    sources = range(taken_ref.shape[0])
    for lanes in range(0, width, TAG):
        totals = [jnp.zeros((taken_ref.shape[1], TAG), F32) for _ in range(out_ref.shape[0])]
        for s in sources:
            tag = taken_ref[s, :, width:].astype(F32)
            value = taken_ref[s, :, lanes : lanes + TAG].astype(F32)
            totals = [t + jnp.where(tag == n + 1, value, 0.0) for n, t in enumerate(totals)]
        for n, total in enumerate(totals):
            out_ref[n, :, lanes : lanes + TAG] = total.astype(BF16)


def product_kernel(chip_ref, *refs):
    *tile_refs, parts_ref, factor_ref, out_ref, panel_ref, high_ref, low_ref, sent_ref = refs
    chunks, blocks, height, half = parts_ref.shape
    for b, ref in enumerate(tile_refs):
        rows = ref.shape[1]
        for k in range(2):
            first = (k * len(tile_refs) + b) * rows
            high_ref[first : first + rows, :], low_ref[first : first + rows, :] = split(ref[k])
    for c in range(chunks):
        for b in range(blocks):
            first = (b * chunks + c) * height
            panel_ref[first : first + height, :] = parts_ref[chip_ref[c], b].astype(F32)
    panel = panel_ref[...].astype(BF16)
    sums = dot(high_ref[...], panel) + dot(low_ref[...], panel)
    gram = dot(factor_ref[...], sums.astype(BF16))
    rows = gram.shape[0] // chunks
    share = sums.shape[0] // 2 // chunks
    sent_ref[:, :rows, :] = gram.reshape(chunks, rows, half)
    sums = sums.reshape(2, chunks, share, half)
    for k in range(2):
        sent_ref[:, rows + k * share : rows + (k + 1) * share, :] = sums[k]
    out_ref[...] = sent_ref[...].astype(BF16)


def total_kernel(arrived_ref, total_ref, copies_ref):
    total = arrived_ref[0].astype(F32)
    for s in range(1, arrived_ref.shape[0]):
        total = total + arrived_ref[s].astype(F32)
    first = copies_ref.shape[1]
    rows = total[:first].astype(BF16)
    for copy in range(copies_ref.shape[0]):
        copies_ref[copy] = rows
    total_ref[...] = total[first:]


def body(front_rows, slot_blocks, inv_factor, ancestor_inv):
    col_count = lax.axis_size("col")
    row_count = lax.axis_size("row")
    chip_count = row_count // 2
    col_index = lax.axis_index("col")
    core = lax.axis_index("row") % 2
    slot_count, chunk_rows, width = front_rows.shape
    half = width // 2
    tile_rows, panel_rows = ancestor_inv.shape
    block_rows = chunk_rows * col_count
    panel_blocks = panel_rows // block_rows
    share = tile_rows // col_count
    diag_width = width // col_count
    same_core = [[2 * j + k for j in range(chip_count)] for k in range(2)]
    core_pairs = [[2 * j, 2 * j + 1] for j in range(chip_count)]
    table = short_routes(chip_count, col_count)
    chip_arg = lax.dynamic_index_in_dim(jnp.asarray(table), col_index, 0, keepdims=False)

    def pair_gather(x):
        return lax.all_gather(x, "row", axis=0, axis_index_groups=core_pairs)

    def over_row(x):
        return lax.all_to_all(x, "row", 0, 0, tiled=True, axis_index_groups=same_core)

    def over_col(x):
        return lax.all_to_all(x, "col", 0, 0, tiled=True)

    factor_cols = lax.dynamic_slice_in_dim(inv_factor, col_index * diag_width, diag_width, 1)
    factor_gram = lax.optimization_barrier(
        lax.dot_general(
            factor_cols,
            inv_factor,
            (((0,), (0,)), ((), ())),
            precision=lax.Precision.HIGHEST,
            preferred_element_type=F32,
        )
    )

    by_panel = pl.pallas_call(
        lambda *refs: scale_kernel(panel_blocks, *refs),
        out_shape=jax.ShapeDtypeStruct((row_count, chunk_rows, half + TAG), BF16),
        in_specs=[SMEM, VMEM, VMEM],
        out_specs=VMEM,
        scratch_shapes=[pltpu.VMEM((slot_count * chunk_rows, width), F32)],
        compiler_params=FETCHING,
    )(
        slot_blocks,
        front_rows.reshape(slot_count * chunk_rows, width),
        inv_factor,
    )
    by_panel, tile = lax.optimization_barrier((by_panel, ancestor_inv))
    tiles = [
        pair_gather(tile[first : first + block_rows])
        for first in range(0, tile_rows - block_rows, block_rows)
    ]
    taken, core, *tiles = lax.optimization_barrier(
        (lax.all_to_all(by_panel, "row", 0, 0, tiled=True), core, *tiles)
    )
    piece = pl.pallas_call(
        place_kernel,
        out_shape=jax.ShapeDtypeStruct((panel_blocks, chunk_rows, half), BF16),
        in_specs=[VMEM],
        out_specs=VMEM,
        compiler_params=PARAMS,
    )(taken)

    route = [
        ((2 * p + k) * col_count + c, (2 * int(table[p, c]) + k) * col_count + p)
        for p in range(col_count)
        for k in range(2)
        for c in range(col_count)
    ]
    piece, tile = lax.optimization_barrier((piece, tile))
    turned = lax.ppermute(piece, ("row", "col"), route)
    factor = over_col(jnp.broadcast_to(piece[None], (col_count, *piece.shape)))
    factor, last_tile = lax.optimization_barrier(
        (factor, pair_gather(tile[tile_rows - block_rows :]))
    )
    tiles.append(last_tile)
    tile_factor = pair_gather(factor)
    tile_factor = tile_factor.transpose(0, 4, 2, 1, 3).reshape(width, 2 * tile_rows)
    parts = over_row(jnp.broadcast_to(turned[None], (chip_count, *turned.shape)))

    sent = (col_count, diag_width + 2 * share, half)
    sent = pl.pallas_call(
        product_kernel,
        out_shape=jax.ShapeDtypeStruct(sent, BF16),
        in_specs=[SMEM] + [VMEM] * (len(tiles) + 2),
        out_specs=VMEM,
        scratch_shapes=[
            pltpu.VMEM((panel_rows, half), F32),
            pltpu.VMEM((2 * tile_rows, panel_rows), BF16),
            pltpu.VMEM((2 * tile_rows, panel_rows), BF16),
            pltpu.VMEM(sent, F32),
        ],
        compiler_params=pltpu.CompilerParams(vmem_limit_bytes=50 * 2**20),
    )(chip_arg, *tiles, parts, tile_factor)
    totals, copies = pl.pallas_call(
        total_kernel,
        out_shape=(
            jax.ShapeDtypeStruct((2 * share, half), F32),
            jax.ShapeDtypeStruct((chip_count, diag_width, half), BF16),
        ),
        in_specs=[VMEM],
        out_specs=(VMEM, VMEM),
        compiler_params=PARAMS,
    )(over_col(sent))
    halves = pair_gather(totals).reshape(2, 2, share, half)
    product = jnp.where(core == 0, halves[:, 0], halves[:, 1])
    product = jnp.concatenate([product[0], product[1]], 1)
    gram_rows = pair_gather(jnp.sum(over_row(copies).astype(F32), axis=0))
    gram_rows = jnp.concatenate([gram_rows[0], gram_rows[1]], 1)
    return (-product, factor_gram + gram_rows)


def solution(mesh):
    in_specs = (P("row", "col", None), P("row"), P(), P("row", "col"))
    out_specs = (P(("row", "col"), None), P("col", None))
    return jax.shard_map(body, mesh=mesh, in_specs=in_specs, out_specs=out_specs, check_vma=False)
```

```python
import itertools

import jax
import jax.numpy as jnp
import numpy as np
from jax import lax
from jax.experimental import pallas as pl
from jax.experimental.pallas import tpu as pltpu
from jax.sharding import PartitionSpec as P

BF16 = jnp.bfloat16
F32 = jnp.float32
TAG = 128
SMEM = pl.BlockSpec(memory_space=pltpu.SMEM)
VMEM = pl.BlockSpec(memory_space=pltpu.VMEM)
ANY = pl.BlockSpec(memory_space=pl.ANY)
PARAMS = pltpu.CompilerParams(vmem_limit_bytes=16 * 2**20)
FETCHING = pltpu.CompilerParams(vmem_limit_bytes=60 * 2**20)


def dot(a, b, dims=((1,), (0,))):
    return lax.dot_general(a, b, (dims, ((), ())), preferred_element_type=F32)


def split(x):
    high = x.astype(BF16)
    return high, (x - high.astype(F32)).astype(BF16)


def chip_position(chip, col, chip_count):
    ys = chip_count // 2
    return chip // ys * 2 + col % 2, chip % ys, col // 2


def hops(a, b, sizes):
    return sum(min((p - q) % n, (q - p) % n) for p, q, n in zip(a, b, sizes))


def short_routes(chip_count, col_count):
    sizes = (4, chip_count // 2, col_count // 2)
    table = np.zeros((col_count, col_count), np.int32)
    for p in range(col_count):
        source = [chip_position(p, c, chip_count) for c in range(col_count)]
        target = [chip_position(j, p, chip_count) for j in range(chip_count)]
        cost = [[hops(s, t, sizes) for t in target] for s in source]
        for limit in itertools.count():
            owner = {}

            def assign(c, seen):
                for j in range(chip_count):
                    if cost[c][j] <= limit and j not in seen:
                        seen.add(j)
                        if j not in owner or assign(owner[j], seen):
                            owner[j] = c
                            return True
                return False

            if all(assign(c, set()) for c in range(col_count)):
                break
        for j, c in owner.items():
            table[p, c] = j
    return table


def scale_kernel(panel_blocks, slots_ref, rows_hbm, factor_hbm, out_ref, rows_ref, factor_ref, scaled_ref, sems):
    half = factor_ref.shape[1] // 2
    parts = [pl.ds(k * half, half) for k in range(2)]
    copies = [pltpu.make_async_copy(rows_hbm, rows_ref, sems.at[0])]
    for k, part in enumerate(parts):
        copies.append(
            pltpu.make_async_copy(factor_hbm.at[part], factor_ref.at[part], sems.at[k + 1])
        )
    for copy in copies:
        copy.start()
    out_ref[...] = jnp.zeros_like(out_ref)
    copies[0].wait()
    for k, part in enumerate(parts):
        copies[k + 1].wait()
        high, low = split(factor_ref[part, :])
        rows = rows_ref[:, part]
        scaled = dot(rows, high) + dot(rows, low)
        scaled_ref[...] = scaled if k == 0 else scaled_ref[...] + scaled
    slot_count = slots_ref.shape[0]
    height = rows_ref.shape[0] // slot_count
    for s in range(slot_count):
        block = slots_ref[s]

        @pl.when(block >= 0)
        def _():
            panel = block // panel_blocks
            number = (block - panel * panel_blocks + 1).astype(F32)
            for k in range(2):
                part = scaled_ref[s * height : (s + 1) * height, k * half : (k + 1) * half]
                out_ref[2 * panel + k, :, :half] = part.astype(BF16)
                out_ref[2 * panel + k, :, half:] = jnp.full((height, TAG), number, F32).astype(BF16)


def place_kernel(taken_ref, out_ref):
    width = taken_ref.shape[2] - TAG
    sources = range(taken_ref.shape[0])
    for lanes in range(0, width, TAG):
        totals = [jnp.zeros((taken_ref.shape[1], TAG), F32) for _ in range(out_ref.shape[0])]
        for s in sources:
            tag = taken_ref[s, :, width:].astype(F32)
            value = taken_ref[s, :, lanes : lanes + TAG].astype(F32)
            totals = [t + jnp.where(tag == n + 1, value, 0.0) for n, t in enumerate(totals)]
        for n, total in enumerate(totals):
            out_ref[n, :, lanes : lanes + TAG] = total.astype(BF16)


def turn_kernel(halves_ref, out_ref, rows_ref):
    _, chunks, blocks, height, half = halves_ref.shape
    for k in range(2):
        for c in range(chunks):
            for b in range(blocks):
                first = (b * chunks + c) * height
                rows_ref[first : first + height, :] = halves_ref[k, c, b].astype(F32)
        out_ref[k * half : (k + 1) * half, :] = rows_ref[...].T.astype(BF16)


def product_kernel(col_ref, chip_ref, *refs):
    *tile_refs, parts_ref, factor_ref, out_ref, panel_ref, high_ref, low_ref, sent_ref = refs
    chunks, blocks, height, half = parts_ref.shape
    for b, ref in enumerate(tile_refs):
        rows = ref.shape[1]
        for k in range(2):
            first = (k * len(tile_refs) + b) * rows
            high_ref[first : first + rows, :], low_ref[first : first + rows, :] = split(ref[k])
    for c in range(chunks):
        for b in range(blocks):
            first = (b * chunks + c) * height
            panel_ref[first : first + height, :] = parts_ref[chip_ref[col_ref[0] * chunks + c], b].astype(F32)
    panel = panel_ref[...].astype(BF16)
    sums = dot(high_ref[...], panel) + dot(low_ref[...], panel)
    gram = dot(factor_ref[...], sums.astype(BF16))
    rows = gram.shape[0] // chunks
    share = sums.shape[0] // 2 // chunks
    sent_ref[:, :rows, :] = gram.reshape(chunks, rows, half)
    sums = sums.reshape(2, chunks, share, half)
    for k in range(2):
        sent_ref[:, rows + k * share : rows + (k + 1) * share, :] = sums[k]
    out_ref[...] = sent_ref[...].astype(BF16)


def total_kernel(arrived_ref, total_ref, copies_ref):
    total = arrived_ref[0].astype(F32)
    for s in range(1, arrived_ref.shape[0]):
        total = total + arrived_ref[s].astype(F32)
    first = copies_ref.shape[1]
    rows = total[:first].astype(BF16)
    for copy in range(copies_ref.shape[0]):
        copies_ref[copy] = rows
    total_ref[...] = total[first:]


def body(front_rows, slot_blocks, inv_factor, ancestor_inv):
    col_count = lax.axis_size("col")
    row_count = lax.axis_size("row")
    chip_count = row_count // 2
    col_index = lax.axis_index("col")
    core = lax.axis_index("row") % 2
    slot_count, chunk_rows, width = front_rows.shape
    half = width // 2
    tile_rows, panel_rows = ancestor_inv.shape
    block_rows = chunk_rows * col_count
    panel_blocks = panel_rows // block_rows
    share = tile_rows // col_count
    diag_width = width // col_count
    same_core = [[2 * j + k for j in range(chip_count)] for k in range(2)]
    core_pairs = [[2 * j, 2 * j + 1] for j in range(chip_count)]
    table = short_routes(chip_count, col_count)
    chip_arg = jnp.asarray(table.reshape(-1))
    col_arg = jnp.reshape(col_index, (1,)).astype(jnp.int32)

    def pair_gather(x):
        return lax.all_gather(x, "row", axis=0, axis_index_groups=core_pairs)

    def over_row(x):
        return lax.all_to_all(x, "row", 0, 0, tiled=True, axis_index_groups=same_core)

    def over_col(x):
        return lax.all_to_all(x, "col", 0, 0, tiled=True)

    factor_cols = lax.dynamic_slice_in_dim(inv_factor, col_index * diag_width, diag_width, 1)
    factor_gram = lax.optimization_barrier(
        lax.dot_general(
            factor_cols,
            inv_factor,
            (((0,), (0,)), ((), ())),
            precision=lax.Precision.HIGHEST,
            preferred_element_type=F32,
        )
    )

    by_panel = pl.pallas_call(
        lambda *refs: scale_kernel(panel_blocks, *refs),
        out_shape=jax.ShapeDtypeStruct((row_count, chunk_rows, half + TAG), BF16),
        in_specs=[SMEM, ANY, ANY],
        out_specs=VMEM,
        scratch_shapes=[
            pltpu.VMEM((slot_count * chunk_rows, width), BF16),
            pltpu.VMEM((width, width), F32),
            pltpu.VMEM((slot_count * chunk_rows, width), F32),
            pltpu.SemaphoreType.DMA((3,)),
        ],
        compiler_params=FETCHING,
    )(
        slot_blocks,
        front_rows.reshape(slot_count * chunk_rows, width),
        inv_factor,
    )
    by_panel, tile = lax.optimization_barrier((by_panel, ancestor_inv))
    tiles = [
        pair_gather(tile[first : first + block_rows])
        for first in range(0, tile_rows - block_rows, block_rows)
    ]
    taken, core, *tiles = lax.optimization_barrier(
        (lax.all_to_all(by_panel, "row", 0, 0, tiled=True), core, *tiles)
    )
    piece = pl.pallas_call(
        place_kernel,
        out_shape=jax.ShapeDtypeStruct((panel_blocks, chunk_rows, half), BF16),
        in_specs=[VMEM],
        out_specs=VMEM,
        compiler_params=PARAMS,
    )(taken)

    route = [
        ((2 * p + k) * col_count + c, (2 * int(table[p, c]) + k) * col_count + p)
        for p in range(col_count)
        for k in range(2)
        for c in range(col_count)
    ]
    piece, tile = lax.optimization_barrier((piece, tile))
    turned = lax.ppermute(piece, ("row", "col"), route)
    factor = over_col(jnp.broadcast_to(piece[None], (col_count, *piece.shape)))
    factor, last_tile = lax.optimization_barrier(
        (factor, pair_gather(tile[tile_rows - block_rows :]))
    )
    tiles.append(last_tile)
    tile_factor = pl.pallas_call(
        turn_kernel,
        out_shape=jax.ShapeDtypeStruct((width, 2 * tile_rows), BF16),
        in_specs=[VMEM],
        out_specs=VMEM,
        scratch_shapes=[pltpu.VMEM((2 * tile_rows, half), F32)],
        compiler_params=PARAMS,
    )(pair_gather(factor))
    parts = over_row(jnp.broadcast_to(turned[None], (chip_count, *turned.shape)))

    sent = (col_count, diag_width + 2 * share, half)
    sent = pl.pallas_call(
        product_kernel,
        out_shape=jax.ShapeDtypeStruct(sent, BF16),
        in_specs=[SMEM, SMEM] + [VMEM] * (len(tiles) + 2),
        out_specs=VMEM,
        scratch_shapes=[
            pltpu.VMEM((panel_rows, half), F32),
            pltpu.VMEM((2 * tile_rows, panel_rows), BF16),
            pltpu.VMEM((2 * tile_rows, panel_rows), BF16),
            pltpu.VMEM(sent, F32),
        ],
        compiler_params=pltpu.CompilerParams(vmem_limit_bytes=50 * 2**20),
    )(col_arg, chip_arg, *tiles, parts, tile_factor)
    totals, copies = pl.pallas_call(
        total_kernel,
        out_shape=(
            jax.ShapeDtypeStruct((2 * share, half), F32),
            jax.ShapeDtypeStruct((chip_count, diag_width, half), BF16),
        ),
        in_specs=[VMEM],
        out_specs=(VMEM, VMEM),
        compiler_params=PARAMS,
    )(over_col(sent))
    halves = pair_gather(totals).reshape(2, 2, share, half)
    product = jnp.where(core == 0, halves[:, 0], halves[:, 1])
    product = jnp.concatenate([product[0], product[1]], 1)
    gram_rows = pair_gather(jnp.sum(over_row(copies).astype(F32), axis=0))
    gram_rows = jnp.concatenate([gram_rows[0], gram_rows[1]], 1)
    return (-product, factor_gram + gram_rows)


def solution(mesh):
    in_specs = (P("row", "col", None), P("row"), P(), P("row", "col"))
    out_specs = (P(("row", "col"), None), P("col", None))
    return jax.shard_map(body, mesh=mesh, in_specs=in_specs, out_specs=out_specs, check_vma=False)
```

```python
import itertools

import jax
import jax.numpy as jnp
import numpy as np
from jax import lax
from jax.experimental import pallas as pl
from jax.experimental.pallas import tpu as pltpu
from jax.sharding import PartitionSpec as P

BF16 = jnp.bfloat16
F32 = jnp.float32
TAG = 128
SMEM = pl.BlockSpec(memory_space=pltpu.SMEM)
VMEM = pl.BlockSpec(memory_space=pltpu.VMEM)
PARAMS = pltpu.CompilerParams(vmem_limit_bytes=16 * 2**20)
FETCHING = pltpu.CompilerParams(vmem_limit_bytes=60 * 2**20)


def dot(a, b, dims=((1,), (0,))):
    return lax.dot_general(a, b, (dims, ((), ())), preferred_element_type=F32)


def split(x):
    high = x.astype(BF16)
    return high, (x - high.astype(F32)).astype(BF16)


def chip_position(chip, col, chip_count):
    ys = chip_count // 2
    return chip // ys * 2 + col % 2, chip % ys, col // 2


def hops(a, b, sizes):
    return sum(min((p - q) % n, (q - p) % n) for p, q, n in zip(a, b, sizes))


def short_routes(chip_count, col_count):
    sizes = (4, chip_count // 2, col_count // 2)
    table = np.zeros((col_count, col_count), np.int32)
    for p in range(col_count):
        source = [chip_position(p, c, chip_count) for c in range(col_count)]
        target = [chip_position(j, p, chip_count) for j in range(chip_count)]
        cost = [[hops(s, t, sizes) for t in target] for s in source]
        for limit in itertools.count():
            owner = {}

            def assign(c, seen):
                for j in range(chip_count):
                    if cost[c][j] <= limit and j not in seen:
                        seen.add(j)
                        if j not in owner or assign(owner[j], seen):
                            owner[j] = c
                            return True
                return False

            if all(assign(c, set()) for c in range(col_count)):
                break
        for j, c in owner.items():
            table[p, c] = j
    return table


def scale_kernel(panel_blocks, slots_ref, rows_ref, factor_ref, out_ref, scaled_ref):
    width = factor_ref.shape[1]
    high, low = split(factor_ref[...])
    rows = rows_ref[...]
    scaled_ref[...] = dot(rows, high) + dot(rows, low)
    out_ref[...] = jnp.zeros_like(out_ref)
    slot_count = slots_ref.shape[0]
    height = rows_ref.shape[0] // slot_count
    for s in range(slot_count):
        block = slots_ref[s]

        @pl.when(block >= 0)
        def _():
            panel = block // panel_blocks
            number = (block - panel * panel_blocks + 1).astype(F32)
            out_ref[panel, :, :width] = scaled_ref[s * height : (s + 1) * height, :].astype(BF16)
            out_ref[panel, :, width:] = jnp.full((height, TAG), number, F32).astype(BF16)


def place_kernel(taken_ref, out_ref):
    width = taken_ref.shape[2] - TAG
    sources = range(taken_ref.shape[0])
    for lanes in range(0, width, TAG):
        totals = [jnp.zeros((taken_ref.shape[1], TAG), F32) for _ in range(out_ref.shape[0])]
        for s in sources:
            tag = taken_ref[s, :, width:].astype(F32)
            value = taken_ref[s, :, lanes : lanes + TAG].astype(F32)
            totals = [t + jnp.where(tag == n + 1, value, 0.0) for n, t in enumerate(totals)]
        for n, total in enumerate(totals):
            out_ref[n, :, lanes : lanes + TAG] = total.astype(BF16)


def merge_kernel(core_ref, pair_ref, piece_ref, copies_ref):
    half = piece_ref.shape[2]

    def merge(first):
        for b in range(piece_ref.shape[0]):
            rows = [pair_ref[k, b, :, first : first + half].astype(F32) for k in range(2)]
            rows = (rows[0] + rows[1]).astype(BF16)
            piece_ref[b] = rows
            for copy in range(copies_ref.shape[0]):
                copies_ref[copy, b] = rows

    @pl.when(core_ref[0] == 0)
    def _():
        merge(0)

    @pl.when(core_ref[0] == 1)
    def _():
        merge(half)


def turn_kernel(halves_ref, out_ref, rows_ref):
    _, chunks, blocks, height, half = halves_ref.shape
    for k in range(2):
        for c in range(chunks):
            for b in range(blocks):
                first = (b * chunks + c) * height
                rows_ref[first : first + height, :] = halves_ref[k, c, b].astype(F32)
        out_ref[k * half : (k + 1) * half, :] = rows_ref[...].T.astype(BF16)


def product_kernel(core_ref, col_ref, chip_ref, own_ref, *refs):
    *tile_refs, parts_ref, factor_ref, out_ref, panel_ref, high_ref, sums_ref, sent_ref = refs
    chunks, blocks, height, half = parts_ref.shape
    tile_rows = own_ref.shape[0]
    for b, ref in enumerate(tile_refs):
        rows = ref.shape[1]
        for k in range(2):
            first = k * tile_rows + b * rows
            high_ref[first : first + rows, :] = ref[k]
    low = split(own_ref[...])[1]
    for c in range(chunks):
        for b in range(blocks):
            first = (b * chunks + c) * height
            panel_ref[first : first + height, :] = parts_ref[chip_ref[col_ref[0] * chunks + c], b].astype(F32)
    panel = panel_ref[...].astype(BF16)
    sums_ref[...] = dot(high_ref[...], panel)
    own = pl.ds(pl.multiple_of(core_ref[0] * tile_rows, tile_rows), tile_rows)
    sums_ref[own, :] = sums_ref[own, :] + dot(low, panel)
    sums = sums_ref[...]
    gram = dot(factor_ref[...], sums.astype(BF16))
    rows = gram.shape[0] // chunks
    share = sums.shape[0] // 2 // chunks
    sent_ref[:, :rows, :] = gram.reshape(chunks, rows, half)
    sums = sums.reshape(2, chunks, share, half)
    for k in range(2):
        sent_ref[:, rows + k * share : rows + (k + 1) * share, :] = sums[k]
    out_ref[...] = sent_ref[...].astype(BF16)


def total_kernel(arrived_ref, total_ref, copies_ref):
    total = arrived_ref[0].astype(F32)
    for s in range(1, arrived_ref.shape[0]):
        total = total + arrived_ref[s].astype(F32)
    first = copies_ref.shape[1]
    rows = total[:first].astype(BF16)
    for copy in range(copies_ref.shape[0]):
        copies_ref[copy] = rows
    total_ref[...] = total[first:]


def body(front_rows, slot_blocks, inv_factor, ancestor_inv):
    col_count = lax.axis_size("col")
    row_count = lax.axis_size("row")
    chip_count = row_count // 2
    col_index = lax.axis_index("col")
    core = lax.axis_index("row") % 2
    slot_count, chunk_rows, width = front_rows.shape
    half = width // 2
    tile_rows, panel_rows = ancestor_inv.shape
    block_rows = chunk_rows * col_count
    panel_blocks = panel_rows // block_rows
    share = tile_rows // col_count
    diag_width = width // col_count
    same_core = [[2 * j + k for j in range(chip_count)] for k in range(2)]
    core_pairs = [[2 * j, 2 * j + 1] for j in range(chip_count)]
    table = short_routes(chip_count, col_count)
    chip_arg = jnp.asarray(table.reshape(-1))
    col_arg = jnp.reshape(col_index, (1,)).astype(jnp.int32)

    def pair_gather(x):
        return lax.all_gather(x, "row", axis=0, axis_index_groups=core_pairs)

    def over_row(x):
        return lax.all_to_all(x, "row", 0, 0, tiled=True, axis_index_groups=same_core)

    def over_col(x):
        return lax.all_to_all(x, "col", 0, 0, tiled=True)

    factor_cols = lax.dynamic_slice_in_dim(inv_factor, col_index * diag_width, diag_width, 1)
    factor_gram = lax.optimization_barrier(
        lax.dot_general(
            factor_cols,
            inv_factor,
            (((0,), (0,)), ((), ())),
            precision=lax.Precision.HIGHEST,
            preferred_element_type=F32,
        )
    )

    by_panel = pl.pallas_call(
        lambda *refs: scale_kernel(panel_blocks, *refs),
        out_shape=jax.ShapeDtypeStruct((chip_count, chunk_rows, width + TAG), BF16),
        in_specs=[SMEM, VMEM, VMEM],
        out_specs=VMEM,
        scratch_shapes=[pltpu.VMEM((slot_count * chunk_rows, width), F32)],
        compiler_params=FETCHING,
    )(
        slot_blocks,
        front_rows.reshape(slot_count * chunk_rows, width),
        inv_factor,
    )
    by_panel, tile = lax.optimization_barrier((by_panel, ancestor_inv))
    high = tile.astype(BF16)
    middle = tile_rows // 2
    taken, core, *tiles = lax.optimization_barrier(
        (over_row(by_panel), core, pair_gather(high[:middle]), pair_gather(high[middle:]))
    )
    core_arg = jnp.reshape(core, (1,)).astype(jnp.int32)
    placed = pl.pallas_call(
        place_kernel,
        out_shape=jax.ShapeDtypeStruct((panel_blocks, chunk_rows, width), BF16),
        in_specs=[VMEM],
        out_specs=VMEM,
        compiler_params=PARAMS,
    )(taken)
    piece, copies = pl.pallas_call(
        merge_kernel,
        out_shape=(
            jax.ShapeDtypeStruct((panel_blocks, chunk_rows, half), BF16),
            jax.ShapeDtypeStruct((col_count, panel_blocks, chunk_rows, half), BF16),
        ),
        in_specs=[SMEM, VMEM],
        out_specs=(VMEM, VMEM),
        compiler_params=PARAMS,
    )(core_arg, pair_gather(placed))

    route = [
        ((2 * p + k) * col_count + c, (2 * int(table[p, c]) + k) * col_count + p)
        for p in range(col_count)
        for k in range(2)
        for c in range(col_count)
    ]
    turned = lax.ppermute(piece, ("row", "col"), route)
    factor = over_col(copies)
    tile_factor = pl.pallas_call(
        turn_kernel,
        out_shape=jax.ShapeDtypeStruct((width, 2 * tile_rows), BF16),
        in_specs=[VMEM],
        out_specs=VMEM,
        scratch_shapes=[pltpu.VMEM((2 * tile_rows, half), F32)],
        compiler_params=PARAMS,
    )(pair_gather(factor))
    parts = over_row(jnp.broadcast_to(turned[None], (chip_count, *turned.shape)))

    sent = (col_count, diag_width + 2 * share, half)
    sent = pl.pallas_call(
        product_kernel,
        out_shape=jax.ShapeDtypeStruct(sent, BF16),
        in_specs=[SMEM, SMEM, SMEM] + [VMEM] * (len(tiles) + 3),
        out_specs=VMEM,
        scratch_shapes=[
            pltpu.VMEM((panel_rows, half), F32),
            pltpu.VMEM((2 * tile_rows, panel_rows), BF16),
            pltpu.VMEM((2 * tile_rows, half), F32),
            pltpu.VMEM(sent, F32),
        ],
        compiler_params=pltpu.CompilerParams(vmem_limit_bytes=24 * 2**20),
    )(core_arg, col_arg, chip_arg, tile, *tiles, parts, tile_factor)
    totals, copies = pl.pallas_call(
        total_kernel,
        out_shape=(
            jax.ShapeDtypeStruct((2 * share, half), F32),
            jax.ShapeDtypeStruct((chip_count, diag_width, half), BF16),
        ),
        in_specs=[VMEM],
        out_specs=(VMEM, VMEM),
        compiler_params=PARAMS,
    )(over_col(sent))
    halves = pair_gather(totals).reshape(2, 2, share, half)
    product = jnp.where(core == 0, halves[:, 0], halves[:, 1])
    product = jnp.concatenate([product[0], product[1]], 1)
    gram_rows = pair_gather(jnp.sum(over_row(copies).astype(F32), axis=0))
    gram_rows = jnp.concatenate([gram_rows[0], gram_rows[1]], 1)
    return (-product, factor_gram + gram_rows)


def solution(mesh):
    in_specs = (P("row", "col", None), P("row"), P(), P("row", "col"))
    out_specs = (P(("row", "col"), None), P("col", None))
    return jax.shard_map(body, mesh=mesh, in_specs=in_specs, out_specs=out_specs, check_vma=False)
```

```python
import itertools

import jax
import jax.numpy as jnp
import numpy as np
from jax import lax
from jax.experimental import pallas as pl
from jax.experimental.pallas import tpu as pltpu
from jax.sharding import PartitionSpec as P

BF16 = jnp.bfloat16
F32 = jnp.float32
TAG = 128
SMEM = pl.BlockSpec(memory_space=pltpu.SMEM)
VMEM = pl.BlockSpec(memory_space=pltpu.VMEM)
PARAMS = pltpu.CompilerParams(vmem_limit_bytes=16 * 2**20)
FETCHING = pltpu.CompilerParams(vmem_limit_bytes=60 * 2**20)


def dot(a, b, dims=((1,), (0,))):
    return lax.dot_general(a, b, (dims, ((), ())), preferred_element_type=F32)


def split(x):
    high = x.astype(BF16)
    return high, (x - high.astype(F32)).astype(BF16)


def chip_position(chip, col, chip_count):
    ys = chip_count // 2
    return chip // ys * 2 + col % 2, chip % ys, col // 2


def hops(a, b, sizes):
    return sum(min((p - q) % n, (q - p) % n) for p, q, n in zip(a, b, sizes))


def short_routes(chip_count, col_count):
    sizes = (4, chip_count // 2, col_count // 2)
    table = np.zeros((col_count, col_count), np.int32)
    for p in range(col_count):
        source = [chip_position(p, c, chip_count) for c in range(col_count)]
        target = [chip_position(j, p, chip_count) for j in range(chip_count)]
        cost = [[hops(s, t, sizes) for t in target] for s in source]
        for limit in itertools.count():
            owner = {}

            def assign(c, seen):
                for j in range(chip_count):
                    if cost[c][j] <= limit and j not in seen:
                        seen.add(j)
                        if j not in owner or assign(owner[j], seen):
                            owner[j] = c
                            return True
                return False

            if all(assign(c, set()) for c in range(col_count)):
                break
        for j, c in owner.items():
            table[p, c] = j
    return table


def scale_kernel(panel_blocks, slots_ref, rows_ref, factor_ref, out_ref, scaled_ref):
    width = factor_ref.shape[1]
    high, low = split(factor_ref[...])
    rows = rows_ref[...]
    scaled_ref[...] = dot(rows, high) + dot(rows, low)
    out_ref[...] = jnp.zeros_like(out_ref)
    slot_count = slots_ref.shape[0]
    height = rows_ref.shape[0] // slot_count
    for s in range(slot_count):
        block = slots_ref[s]

        @pl.when(block >= 0)
        def _():
            panel = block // panel_blocks
            number = (block - panel * panel_blocks + 1).astype(F32)
            out_ref[panel, :, :width] = scaled_ref[s * height : (s + 1) * height, :].astype(BF16)
            out_ref[panel, :, width:] = jnp.full((height, TAG), number, F32).astype(BF16)


def place_kernel(taken_ref, out_ref):
    width = taken_ref.shape[2] - TAG
    sources = range(taken_ref.shape[0])
    for lanes in range(0, width, TAG):
        totals = [jnp.zeros((taken_ref.shape[1], TAG), F32) for _ in range(out_ref.shape[0])]
        for s in sources:
            tag = taken_ref[s, :, width:].astype(F32)
            value = taken_ref[s, :, lanes : lanes + TAG].astype(F32)
            totals = [t + jnp.where(tag == n + 1, value, 0.0) for n, t in enumerate(totals)]
        for n, total in enumerate(totals):
            out_ref[n, :, lanes : lanes + TAG] = total.astype(BF16)


def merge_kernel(core_ref, pair_ref, piece_ref, copies_ref):
    half = piece_ref.shape[2]

    def merge(first):
        for b in range(piece_ref.shape[0]):
            rows = [pair_ref[k, b, :, first : first + half].astype(F32) for k in range(2)]
            rows = (rows[0] + rows[1]).astype(BF16)
            piece_ref[b] = rows
            for copy in range(copies_ref.shape[0]):
                copies_ref[copy, b] = rows

    @pl.when(core_ref[0] == 0)
    def _():
        merge(0)

    @pl.when(core_ref[0] == 1)
    def _():
        merge(half)


def turn_kernel(halves_ref, out_ref, rows_ref):
    _, chunks, blocks, height, half = halves_ref.shape
    for k in range(2):
        for c in range(chunks):
            for b in range(blocks):
                first = (b * chunks + c) * height
                rows_ref[first : first + height, :] = halves_ref[k, c, b].astype(F32)
        out_ref[k * half : (k + 1) * half, :] = rows_ref[...].T.astype(BF16)


def product_kernel(core_ref, col_ref, chip_ref, own_ref, *refs):
    *tile_refs, parts_ref, factor_ref, out_ref, panel_ref, high_ref, sums_ref, sent_ref = refs
    chunks, blocks, height, half = parts_ref.shape
    tile_rows = own_ref.shape[0]
    for b, ref in enumerate(tile_refs):
        rows = ref.shape[1]
        for k in range(2):
            first = k * tile_rows + b * rows
            high_ref[first : first + rows, :] = ref[k]
    low = split(own_ref[...])[1]
    for c in range(chunks):
        for b in range(blocks):
            first = (b * chunks + c) * height
            panel_ref[first : first + height, :] = parts_ref[chip_ref[col_ref[0] * chunks + c], b].astype(F32)
    panel = panel_ref[...].astype(BF16)
    sums_ref[...] = dot(high_ref[...], panel)
    own = pl.ds(pl.multiple_of(core_ref[0] * tile_rows, tile_rows), tile_rows)
    sums_ref[own, :] = sums_ref[own, :] + dot(low, panel)
    sums = sums_ref[...]
    gram = dot(factor_ref[...], sums.astype(BF16))
    rows = gram.shape[0] // chunks
    share = sums.shape[0] // 2 // chunks
    sent_ref[:, :rows, :] = gram.reshape(chunks, rows, half)
    sums = sums.reshape(2, chunks, share, half)
    for k in range(2):
        sent_ref[:, rows + k * share : rows + (k + 1) * share, :] = sums[k]
    out_ref[...] = sent_ref[...].astype(BF16)


def total_kernel(arrived_ref, total_ref, copies_ref):
    total = arrived_ref[0].astype(F32)
    for s in range(1, arrived_ref.shape[0]):
        total = total + arrived_ref[s].astype(F32)
    first = copies_ref.shape[1]
    rows = total[:first].astype(BF16)
    for copy in range(copies_ref.shape[0]):
        copies_ref[copy] = rows
    total_ref[...] = total[first:]


def body(front_rows, slot_blocks, inv_factor, ancestor_inv):
    col_count = lax.axis_size("col")
    row_count = lax.axis_size("row")
    chip_count = row_count // 2
    col_index = lax.axis_index("col")
    core = lax.axis_index("row") % 2
    slot_count, chunk_rows, width = front_rows.shape
    half = width // 2
    tile_rows, panel_rows = ancestor_inv.shape
    block_rows = chunk_rows * col_count
    panel_blocks = panel_rows // block_rows
    share = tile_rows // col_count
    diag_width = width // col_count
    same_core = [[2 * j + k for j in range(chip_count)] for k in range(2)]
    core_pairs = [[2 * j, 2 * j + 1] for j in range(chip_count)]
    table = short_routes(chip_count, col_count)
    chip_arg = jnp.asarray(table.reshape(-1))
    col_arg = jnp.reshape(col_index, (1,)).astype(jnp.int32)

    def pair_gather(x):
        return lax.all_gather(x, "row", axis=0, axis_index_groups=core_pairs)

    def over_row(x):
        return lax.all_to_all(x, "row", 0, 0, tiled=True, axis_index_groups=same_core)

    def over_col(x):
        return lax.all_to_all(x, "col", 0, 0, tiled=True)

    factor_cols = lax.dynamic_slice_in_dim(inv_factor, col_index * diag_width, diag_width, 1)
    factor_gram = lax.optimization_barrier(
        lax.dot_general(
            factor_cols,
            inv_factor,
            (((0,), (0,)), ((), ())),
            precision=lax.Precision.HIGHEST,
            preferred_element_type=F32,
        )
    )

    by_panel = pl.pallas_call(
        lambda *refs: scale_kernel(panel_blocks, *refs),
        out_shape=jax.ShapeDtypeStruct((chip_count, chunk_rows, width + TAG), BF16),
        in_specs=[SMEM, VMEM, VMEM],
        out_specs=VMEM,
        scratch_shapes=[pltpu.VMEM((slot_count * chunk_rows, width), F32)],
        compiler_params=FETCHING,
    )(
        slot_blocks,
        front_rows.reshape(slot_count * chunk_rows, width),
        inv_factor,
    )
    by_panel, tile = lax.optimization_barrier((by_panel, ancestor_inv))
    high = tile.astype(BF16)
    middle = tile_rows // 2
    taken, core, first_half = lax.optimization_barrier(
        (over_row(by_panel), core, pair_gather(high[:middle]))
    )
    core_arg = jnp.reshape(core, (1,)).astype(jnp.int32)
    placed = pl.pallas_call(
        place_kernel,
        out_shape=jax.ShapeDtypeStruct((panel_blocks, chunk_rows, width), BF16),
        in_specs=[VMEM],
        out_specs=VMEM,
        compiler_params=PARAMS,
    )(taken)
    piece, copies = pl.pallas_call(
        merge_kernel,
        out_shape=(
            jax.ShapeDtypeStruct((panel_blocks, chunk_rows, half), BF16),
            jax.ShapeDtypeStruct((col_count, panel_blocks, chunk_rows, half), BF16),
        ),
        in_specs=[SMEM, VMEM],
        out_specs=(VMEM, VMEM),
        compiler_params=PARAMS,
    )(core_arg, pair_gather(placed))

    route = [
        ((2 * p + k) * col_count + c, (2 * int(table[p, c]) + k) * col_count + p)
        for p in range(col_count)
        for k in range(2)
        for c in range(col_count)
    ]
    turned = lax.ppermute(piece, ("row", "col"), route)
    factor, second_half = lax.optimization_barrier((over_col(copies), pair_gather(high[middle:])))
    tiles = [first_half, second_half]
    tile_factor = pl.pallas_call(
        turn_kernel,
        out_shape=jax.ShapeDtypeStruct((width, 2 * tile_rows), BF16),
        in_specs=[VMEM],
        out_specs=VMEM,
        scratch_shapes=[pltpu.VMEM((2 * tile_rows, half), F32)],
        compiler_params=PARAMS,
    )(pair_gather(factor))
    parts = over_row(jnp.broadcast_to(turned[None], (chip_count, *turned.shape)))

    sent = (col_count, diag_width + 2 * share, half)
    sent = pl.pallas_call(
        product_kernel,
        out_shape=jax.ShapeDtypeStruct(sent, BF16),
        in_specs=[SMEM, SMEM, SMEM] + [VMEM] * (len(tiles) + 3),
        out_specs=VMEM,
        scratch_shapes=[
            pltpu.VMEM((panel_rows, half), F32),
            pltpu.VMEM((2 * tile_rows, panel_rows), BF16),
            pltpu.VMEM((2 * tile_rows, half), F32),
            pltpu.VMEM(sent, F32),
        ],
        compiler_params=pltpu.CompilerParams(vmem_limit_bytes=24 * 2**20),
    )(core_arg, col_arg, chip_arg, tile, *tiles, parts, tile_factor)
    totals, copies = pl.pallas_call(
        total_kernel,
        out_shape=(
            jax.ShapeDtypeStruct((2 * share, half), F32),
            jax.ShapeDtypeStruct((chip_count, diag_width, half), BF16),
        ),
        in_specs=[VMEM],
        out_specs=(VMEM, VMEM),
        compiler_params=PARAMS,
    )(over_col(sent))
    halves = pair_gather(totals).reshape(2, 2, share, half)
    product = jnp.where(core == 0, halves[:, 0], halves[:, 1])
    product = jnp.concatenate([product[0], product[1]], 1)
    gram_rows = pair_gather(jnp.sum(over_row(copies).astype(F32), axis=0))
    gram_rows = jnp.concatenate([gram_rows[0], gram_rows[1]], 1)
    return (-product, factor_gram + gram_rows)


def solution(mesh):
    in_specs = (P("row", "col", None), P("row"), P(), P("row", "col"))
    out_specs = (P(("row", "col"), None), P("col", None))
    return jax.shard_map(body, mesh=mesh, in_specs=in_specs, out_specs=out_specs, check_vma=False)
```

```python
import itertools

import jax
import jax.numpy as jnp
import numpy as np
from jax import lax
from jax.experimental import pallas as pl
from jax.experimental.pallas import tpu as pltpu
from jax.sharding import PartitionSpec as P

BF16 = jnp.bfloat16
F32 = jnp.float32
TAG = 128
SMEM = pl.BlockSpec(memory_space=pltpu.SMEM)
VMEM = pl.BlockSpec(memory_space=pltpu.VMEM)
PARAMS = pltpu.CompilerParams(vmem_limit_bytes=16 * 2**20)
FETCHING = pltpu.CompilerParams(vmem_limit_bytes=60 * 2**20)


def dot(a, b, dims=((1,), (0,))):
    return lax.dot_general(a, b, (dims, ((), ())), preferred_element_type=F32)


def split(x):
    high = x.astype(BF16)
    return high, (x - high.astype(F32)).astype(BF16)


def chip_position(chip, col, chip_count):
    ys = chip_count // 2
    return chip // ys * 2 + col % 2, chip % ys, col // 2


def hops(a, b, sizes):
    return sum(min((p - q) % n, (q - p) % n) for p, q, n in zip(a, b, sizes))


def short_routes(chip_count, col_count):
    sizes = (4, chip_count // 2, col_count // 2)
    table = np.zeros((col_count, col_count), np.int32)
    for p in range(col_count):
        source = [chip_position(p, c, chip_count) for c in range(col_count)]
        target = [chip_position(j, p, chip_count) for j in range(chip_count)]
        cost = [[hops(s, t, sizes) for t in target] for s in source]
        for limit in itertools.count():
            owner = {}

            def assign(c, seen):
                for j in range(chip_count):
                    if cost[c][j] <= limit and j not in seen:
                        seen.add(j)
                        if j not in owner or assign(owner[j], seen):
                            owner[j] = c
                            return True
                return False

            if all(assign(c, set()) for c in range(col_count)):
                break
        for j, c in owner.items():
            table[p, c] = j
    return table


def scale_kernel(panel_blocks, slots_ref, rows_ref, factor_ref, out_ref, scaled_ref):
    half = factor_ref.shape[1] // 2
    high, low = split(factor_ref[...])
    rows = rows_ref[...]
    scaled_ref[...] = dot(rows, high) + dot(rows, low)
    out_ref[...] = jnp.zeros_like(out_ref)
    slot_count = slots_ref.shape[0]
    height = rows_ref.shape[0] // slot_count
    for s in range(slot_count):
        block = slots_ref[s]

        @pl.when(block >= 0)
        def _():
            panel = block // panel_blocks
            number = (block - panel * panel_blocks + 1).astype(F32)
            for k in range(2):
                part = scaled_ref[s * height : (s + 1) * height, k * half : (k + 1) * half]
                out_ref[2 * panel + k, :, :half] = part.astype(BF16)
                out_ref[2 * panel + k, :, half:] = jnp.full((height, TAG), number, F32).astype(BF16)


def place_kernel(taken_ref, out_ref, copies_ref):
    width = taken_ref.shape[2] - TAG
    sources = range(taken_ref.shape[0])
    for lanes in range(0, width, TAG):
        totals = [jnp.zeros((taken_ref.shape[1], TAG), F32) for _ in range(out_ref.shape[0])]
        for s in sources:
            tag = taken_ref[s, :, width:].astype(F32)
            value = taken_ref[s, :, lanes : lanes + TAG].astype(F32)
            totals = [t + jnp.where(tag == n + 1, value, 0.0) for n, t in enumerate(totals)]
        for n, total in enumerate(totals):
            rows = total.astype(BF16)
            out_ref[n, :, lanes : lanes + TAG] = rows
            for copy in range(copies_ref.shape[0]):
                copies_ref[copy, n, :, lanes : lanes + TAG] = rows


def turn_kernel(halves_ref, out_ref, rows_ref):
    _, chunks, blocks, height, half = halves_ref.shape
    for k in range(2):
        for c in range(chunks):
            for b in range(blocks):
                first = (b * chunks + c) * height
                rows_ref[first : first + height, :] = halves_ref[k, c, b].astype(F32)
        out_ref[k * half : (k + 1) * half, :] = rows_ref[...].T.astype(BF16)


def product_kernel(core_ref, col_ref, chip_ref, own_ref, *refs):
    *tile_refs, parts_ref, factor_ref, out_ref, panel_ref, high_ref, sums_ref, sent_ref = refs
    chunks, blocks, height, half = parts_ref.shape
    tile_rows = own_ref.shape[0]
    for b, ref in enumerate(tile_refs):
        rows = ref.shape[1]
        for k in range(2):
            first = k * tile_rows + b * rows
            high_ref[first : first + rows, :] = ref[k]
    low = split(own_ref[...])[1]
    for c in range(chunks):
        for b in range(blocks):
            first = (b * chunks + c) * height
            panel_ref[first : first + height, :] = parts_ref[chip_ref[col_ref[0] * chunks + c], b].astype(F32)
    panel = panel_ref[...].astype(BF16)
    sums_ref[...] = dot(high_ref[...], panel)
    own = pl.ds(pl.multiple_of(core_ref[0] * tile_rows, tile_rows), tile_rows)
    sums_ref[own, :] = sums_ref[own, :] + dot(low, panel)
    sums = sums_ref[...]
    gram = dot(factor_ref[...], sums.astype(BF16))
    rows = gram.shape[0] // chunks
    share = sums.shape[0] // 2 // chunks
    sent_ref[:, :rows, :] = gram.reshape(chunks, rows, half)
    sums = sums.reshape(2, chunks, share, half)
    for k in range(2):
        sent_ref[:, rows + k * share : rows + (k + 1) * share, :] = sums[k]
    out_ref[...] = sent_ref[...].astype(BF16)


def total_kernel(arrived_ref, total_ref, copies_ref):
    total = arrived_ref[0].astype(F32)
    for s in range(1, arrived_ref.shape[0]):
        total = total + arrived_ref[s].astype(F32)
    first = copies_ref.shape[1]
    rows = total[:first].astype(BF16)
    for copy in range(copies_ref.shape[0]):
        copies_ref[copy] = rows
    total_ref[...] = total[first:]


def body(front_rows, slot_blocks, inv_factor, ancestor_inv):
    col_count = lax.axis_size("col")
    row_count = lax.axis_size("row")
    chip_count = row_count // 2
    col_index = lax.axis_index("col")
    core = lax.axis_index("row") % 2
    slot_count, chunk_rows, width = front_rows.shape
    half = width // 2
    tile_rows, panel_rows = ancestor_inv.shape
    block_rows = chunk_rows * col_count
    panel_blocks = panel_rows // block_rows
    share = tile_rows // col_count
    diag_width = width // col_count
    same_core = [[2 * j + k for j in range(chip_count)] for k in range(2)]
    core_pairs = [[2 * j, 2 * j + 1] for j in range(chip_count)]
    table = short_routes(chip_count, col_count)
    chip_arg = jnp.asarray(table.reshape(-1))
    col_arg = jnp.reshape(col_index, (1,)).astype(jnp.int32)

    def pair_gather(x):
        return lax.all_gather(x, "row", axis=0, axis_index_groups=core_pairs)

    def over_row(x):
        return lax.all_to_all(x, "row", 0, 0, tiled=True, axis_index_groups=same_core)

    def over_col(x):
        return lax.all_to_all(x, "col", 0, 0, tiled=True)

    factor_cols = lax.dynamic_slice_in_dim(inv_factor, col_index * diag_width, diag_width, 1)
    factor_gram = lax.optimization_barrier(
        lax.dot_general(
            factor_cols,
            inv_factor,
            (((0,), (0,)), ((), ())),
            precision=lax.Precision.HIGHEST,
            preferred_element_type=F32,
        )
    )

    by_panel = pl.pallas_call(
        lambda *refs: scale_kernel(panel_blocks, *refs),
        out_shape=jax.ShapeDtypeStruct((row_count, chunk_rows, half + TAG), BF16),
        in_specs=[SMEM, VMEM, VMEM],
        out_specs=VMEM,
        scratch_shapes=[pltpu.VMEM((slot_count * chunk_rows, width), F32)],
        compiler_params=FETCHING,
    )(
        slot_blocks,
        front_rows.reshape(slot_count * chunk_rows, width),
        inv_factor,
    )
    by_panel, tile = lax.optimization_barrier((by_panel, ancestor_inv))
    high = tile.astype(BF16)
    middle = tile_rows // 2
    taken, core, first_half = lax.optimization_barrier(
        (
            lax.all_to_all(by_panel, "row", 0, 0, tiled=True),
            core,
            pair_gather(high[:middle]),
        )
    )
    core_arg = jnp.reshape(core, (1,)).astype(jnp.int32)
    piece, copies = pl.pallas_call(
        place_kernel,
        out_shape=(
            jax.ShapeDtypeStruct((panel_blocks, chunk_rows, half), BF16),
            jax.ShapeDtypeStruct((col_count, panel_blocks, chunk_rows, half), BF16),
        ),
        in_specs=[VMEM],
        out_specs=(VMEM, VMEM),
        compiler_params=PARAMS,
    )(taken)

    route = [
        ((2 * p + k) * col_count + c, (2 * int(table[p, c]) + k) * col_count + p)
        for p in range(col_count)
        for k in range(2)
        for c in range(col_count)
    ]
    turned = lax.ppermute(piece, ("row", "col"), route)
    factor, second_half = lax.optimization_barrier((over_col(copies), pair_gather(high[middle:])))
    tiles = [first_half, second_half]
    tile_factor = pl.pallas_call(
        turn_kernel,
        out_shape=jax.ShapeDtypeStruct((width, 2 * tile_rows), BF16),
        in_specs=[VMEM],
        out_specs=VMEM,
        scratch_shapes=[pltpu.VMEM((2 * tile_rows, half), F32)],
        compiler_params=PARAMS,
    )(pair_gather(factor))
    parts = over_row(jnp.broadcast_to(turned[None], (chip_count, *turned.shape)))

    sent = (col_count, diag_width + 2 * share, half)
    sent = pl.pallas_call(
        product_kernel,
        out_shape=jax.ShapeDtypeStruct(sent, BF16),
        in_specs=[SMEM, SMEM, SMEM] + [VMEM] * (len(tiles) + 3),
        out_specs=VMEM,
        scratch_shapes=[
            pltpu.VMEM((panel_rows, half), F32),
            pltpu.VMEM((2 * tile_rows, panel_rows), BF16),
            pltpu.VMEM((2 * tile_rows, half), F32),
            pltpu.VMEM(sent, F32),
        ],
        compiler_params=pltpu.CompilerParams(vmem_limit_bytes=24 * 2**20),
    )(core_arg, col_arg, chip_arg, tile, *tiles, parts, tile_factor)
    totals, copies = pl.pallas_call(
        total_kernel,
        out_shape=(
            jax.ShapeDtypeStruct((2 * share, half), F32),
            jax.ShapeDtypeStruct((chip_count, diag_width, half), BF16),
        ),
        in_specs=[VMEM],
        out_specs=(VMEM, VMEM),
        compiler_params=PARAMS,
    )(over_col(sent))
    halves = pair_gather(totals).reshape(2, 2, share, half)
    product = jnp.where(core == 0, halves[:, 0], halves[:, 1])
    product = jnp.concatenate([product[0], product[1]], 1)
    gram_rows = pair_gather(jnp.sum(over_row(copies).astype(F32), axis=0))
    gram_rows = jnp.concatenate([gram_rows[0], gram_rows[1]], 1)
    return (-product, factor_gram + gram_rows)


def solution(mesh):
    in_specs = (P("row", "col", None), P("row"), P(), P("row", "col"))
    out_specs = (P(("row", "col"), None), P("col", None))
    return jax.shard_map(body, mesh=mesh, in_specs=in_specs, out_specs=out_specs, check_vma=False)
```

```python
import itertools

import jax
import jax.numpy as jnp
import numpy as np
from jax import lax
from jax.experimental import pallas as pl
from jax.experimental.pallas import tpu as pltpu
from jax.sharding import PartitionSpec as P

BF16 = jnp.bfloat16
F32 = jnp.float32
TAG = 128
SMEM = pl.BlockSpec(memory_space=pltpu.SMEM)
VMEM = pl.BlockSpec(memory_space=pltpu.VMEM)
PARAMS = pltpu.CompilerParams(vmem_limit_bytes=16 * 2**20)
FETCHING = pltpu.CompilerParams(vmem_limit_bytes=60 * 2**20)


def dot(a, b, dims=((1,), (0,))):
    return lax.dot_general(a, b, (dims, ((), ())), preferred_element_type=F32)


def split(x):
    high = x.astype(BF16)
    return high, (x - high.astype(F32)).astype(BF16)


def chip_position(chip, col, chip_count):
    ys = chip_count // 2
    return chip // ys * 2 + col % 2, chip % ys, col // 2


def hops(a, b, sizes):
    return sum(min((p - q) % n, (q - p) % n) for p, q, n in zip(a, b, sizes))


def short_routes(chip_count, col_count):
    sizes = (4, chip_count // 2, col_count // 2)
    table = np.zeros((col_count, col_count), np.int32)
    for p in range(col_count):
        source = [chip_position(p, c, chip_count) for c in range(col_count)]
        target = [chip_position(j, p, chip_count) for j in range(chip_count)]
        cost = [[hops(s, t, sizes) for t in target] for s in source]
        for limit in itertools.count():
            owner = {}

            def assign(c, seen):
                for j in range(chip_count):
                    if cost[c][j] <= limit and j not in seen:
                        seen.add(j)
                        if j not in owner or assign(owner[j], seen):
                            owner[j] = c
                            return True
                return False

            if all(assign(c, set()) for c in range(col_count)):
                break
        for j, c in owner.items():
            table[p, c] = j
    return table


def scale_kernel(panel_blocks, slots_ref, rows_ref, factor_ref, out_ref, scaled_ref):
    half = factor_ref.shape[1] // 2
    high, low = split(factor_ref[...])
    rows = rows_ref[...]
    scaled_ref[...] = dot(rows, high) + dot(rows, low)
    out_ref[...] = jnp.zeros_like(out_ref)
    slot_count = slots_ref.shape[0]
    height = rows_ref.shape[0] // slot_count
    for s in range(slot_count):
        block = slots_ref[s]

        @pl.when(block >= 0)
        def _():
            panel = block // panel_blocks
            number = (block - panel * panel_blocks + 1).astype(F32)
            for k in range(2):
                part = scaled_ref[s * height : (s + 1) * height, k * half : (k + 1) * half]
                out_ref[2 * panel + k, :, :half] = part.astype(BF16)
                out_ref[2 * panel + k, :, half:] = jnp.full((height, TAG), number, F32).astype(BF16)


def place_kernel(taken_ref, out_ref, copies_ref):
    width = taken_ref.shape[2] - TAG
    sources = range(taken_ref.shape[0])
    for lanes in range(0, width, TAG):
        totals = [jnp.zeros((taken_ref.shape[1], TAG), F32) for _ in range(out_ref.shape[0])]
        for s in sources:
            tag = taken_ref[s, :, width:].astype(F32)
            value = taken_ref[s, :, lanes : lanes + TAG].astype(F32)
            totals = [t + jnp.where(tag == n + 1, value, 0.0) for n, t in enumerate(totals)]
        for n, total in enumerate(totals):
            rows = total.astype(BF16)
            out_ref[n, :, lanes : lanes + TAG] = rows
            for copy in range(copies_ref.shape[0]):
                copies_ref[copy, n, :, lanes : lanes + TAG] = rows


def product_kernel(chip_ref, *refs):
    *tile_refs, parts_ref, factor_ref, out_ref, panel_ref, high_ref, low_ref, sent_ref = refs
    chunks, blocks, height, half = parts_ref.shape
    for b, ref in enumerate(tile_refs):
        rows = ref.shape[1]
        for k in range(2):
            first = (k * len(tile_refs) + b) * rows
            high_ref[first : first + rows, :], low_ref[first : first + rows, :] = split(ref[k])
    for c in range(chunks):
        for b in range(blocks):
            first = (b * chunks + c) * height
            panel_ref[first : first + height, :] = parts_ref[chip_ref[c], b].astype(F32)
    panel = panel_ref[...].astype(BF16)
    sums = dot(high_ref[...], panel) + dot(low_ref[...], panel)
    gram = dot(factor_ref[...], sums.astype(BF16))
    rows = gram.shape[0] // chunks
    share = sums.shape[0] // 2 // chunks
    sent_ref[:, :rows, :] = gram.reshape(chunks, rows, half)
    sums = sums.reshape(2, chunks, share, half)
    for k in range(2):
        sent_ref[:, rows + k * share : rows + (k + 1) * share, :] = sums[k]
    out_ref[...] = sent_ref[...].astype(BF16)


def total_kernel(arrived_ref, total_ref, copies_ref):
    total = arrived_ref[0].astype(F32)
    for s in range(1, arrived_ref.shape[0]):
        total = total + arrived_ref[s].astype(F32)
    first = copies_ref.shape[1]
    rows = total[:first].astype(BF16)
    for copy in range(copies_ref.shape[0]):
        copies_ref[copy] = rows
    total_ref[...] = total[first:]


def body(front_rows, slot_blocks, inv_factor, ancestor_inv):
    col_count = lax.axis_size("col")
    row_count = lax.axis_size("row")
    chip_count = row_count // 2
    col_index = lax.axis_index("col")
    core = lax.axis_index("row") % 2
    slot_count, chunk_rows, width = front_rows.shape
    half = width // 2
    tile_rows, panel_rows = ancestor_inv.shape
    block_rows = chunk_rows * col_count
    panel_blocks = panel_rows // block_rows
    share = tile_rows // col_count
    diag_width = width // col_count
    same_core = [[2 * j + k for j in range(chip_count)] for k in range(2)]
    core_pairs = [[2 * j, 2 * j + 1] for j in range(chip_count)]
    table = short_routes(chip_count, col_count)
    chip_arg = lax.dynamic_index_in_dim(jnp.asarray(table), col_index, 0, keepdims=False)

    def pair_gather(x):
        return lax.all_gather(x, "row", axis=0, axis_index_groups=core_pairs)

    def over_row(x):
        return lax.all_to_all(x, "row", 0, 0, tiled=True, axis_index_groups=same_core)

    def over_col(x):
        return lax.all_to_all(x, "col", 0, 0, tiled=True)

    factor_cols = lax.dynamic_slice_in_dim(inv_factor, col_index * diag_width, diag_width, 1)
    factor_gram = lax.optimization_barrier(
        lax.dot_general(
            factor_cols,
            inv_factor,
            (((0,), (0,)), ((), ())),
            precision=lax.Precision.HIGHEST,
            preferred_element_type=F32,
        )
    )

    by_panel = pl.pallas_call(
        lambda *refs: scale_kernel(panel_blocks, *refs),
        out_shape=jax.ShapeDtypeStruct((row_count, chunk_rows, half + TAG), BF16),
        in_specs=[SMEM, VMEM, VMEM],
        out_specs=VMEM,
        scratch_shapes=[pltpu.VMEM((slot_count * chunk_rows, width), F32)],
        compiler_params=FETCHING,
    )(
        slot_blocks,
        front_rows.reshape(slot_count * chunk_rows, width),
        inv_factor,
    )
    by_panel, tile = lax.optimization_barrier((by_panel, ancestor_inv))
    tiles = [
        pair_gather(tile[first : first + block_rows])
        for first in range(0, tile_rows - block_rows, block_rows)
    ]
    taken, core, *tiles = lax.optimization_barrier(
        (lax.all_to_all(by_panel, "row", 0, 0, tiled=True), core, *tiles)
    )
    piece, copies = pl.pallas_call(
        place_kernel,
        out_shape=(
            jax.ShapeDtypeStruct((panel_blocks, chunk_rows, half), BF16),
            jax.ShapeDtypeStruct((col_count, panel_blocks, chunk_rows, half), BF16),
        ),
        in_specs=[VMEM],
        out_specs=(VMEM, VMEM),
        compiler_params=PARAMS,
    )(taken)

    route = [
        ((2 * p + k) * col_count + c, (2 * int(table[p, c]) + k) * col_count + p)
        for p in range(col_count)
        for k in range(2)
        for c in range(col_count)
    ]
    piece, copies, tile = lax.optimization_barrier((piece, copies, tile))
    turned = lax.ppermute(piece, ("row", "col"), route)
    factor = over_col(copies)
    factor, last_tile = lax.optimization_barrier(
        (factor, pair_gather(tile[tile_rows - block_rows :]))
    )
    tiles.append(last_tile)
    tile_factor = pair_gather(factor)
    tile_factor = tile_factor.transpose(0, 4, 2, 1, 3).reshape(width, 2 * tile_rows)
    parts = over_row(jnp.broadcast_to(turned[None], (chip_count, *turned.shape)))

    sent = (col_count, diag_width + 2 * share, half)
    sent = pl.pallas_call(
        product_kernel,
        out_shape=jax.ShapeDtypeStruct(sent, BF16),
        in_specs=[SMEM] + [VMEM] * (len(tiles) + 2),
        out_specs=VMEM,
        scratch_shapes=[
            pltpu.VMEM((panel_rows, half), F32),
            pltpu.VMEM((2 * tile_rows, panel_rows), BF16),
            pltpu.VMEM((2 * tile_rows, panel_rows), BF16),
            pltpu.VMEM(sent, F32),
        ],
        compiler_params=pltpu.CompilerParams(vmem_limit_bytes=50 * 2**20),
    )(chip_arg, *tiles, parts, tile_factor)
    totals, copies = pl.pallas_call(
        total_kernel,
        out_shape=(
            jax.ShapeDtypeStruct((2 * share, half), F32),
            jax.ShapeDtypeStruct((chip_count, diag_width, half), BF16),
        ),
        in_specs=[VMEM],
        out_specs=(VMEM, VMEM),
        compiler_params=PARAMS,
    )(over_col(sent))
    halves = pair_gather(totals).reshape(2, 2, share, half)
    product = jnp.where(core == 0, halves[:, 0], halves[:, 1])
    product = jnp.concatenate([product[0], product[1]], 1)
    gram_rows = pair_gather(jnp.sum(over_row(copies).astype(F32), axis=0))
    gram_rows = jnp.concatenate([gram_rows[0], gram_rows[1]], 1)
    return (-product, factor_gram + gram_rows)


def solution(mesh):
    in_specs = (P("row", "col", None), P("row"), P(), P("row", "col"))
    out_specs = (P(("row", "col"), None), P("col", None))
    return jax.shard_map(body, mesh=mesh, in_specs=in_specs, out_specs=out_specs, check_vma=False)
```

```python
import itertools

import jax
import jax.numpy as jnp
import numpy as np
from jax import lax
from jax.experimental import pallas as pl
from jax.experimental.pallas import tpu as pltpu
from jax.sharding import PartitionSpec as P

BF16 = jnp.bfloat16
F32 = jnp.float32
TAG = 128
SMEM = pl.BlockSpec(memory_space=pltpu.SMEM)
VMEM = pl.BlockSpec(memory_space=pltpu.VMEM)
PARAMS = pltpu.CompilerParams(vmem_limit_bytes=16 * 2**20)
FETCHING = pltpu.CompilerParams(vmem_limit_bytes=60 * 2**20)


def dot(a, b, dims=((1,), (0,))):
    return lax.dot_general(a, b, (dims, ((), ())), preferred_element_type=F32)


def split(x):
    high = x.astype(BF16)
    return high, (x - high.astype(F32)).astype(BF16)


def chip_position(chip, col, chip_count):
    ys = chip_count // 2
    return chip // ys * 2 + col % 2, chip % ys, col // 2


def hops(a, b, sizes):
    return sum(min((p - q) % n, (q - p) % n) for p, q, n in zip(a, b, sizes))


def short_routes(chip_count, col_count):
    sizes = (4, chip_count // 2, col_count // 2)
    table = np.zeros((col_count, col_count), np.int32)
    for p in range(col_count):
        source = [chip_position(p, c, chip_count) for c in range(col_count)]
        target = [chip_position(j, p, chip_count) for j in range(chip_count)]
        cost = [[hops(s, t, sizes) for t in target] for s in source]
        for limit in itertools.count():
            owner = {}

            def assign(c, seen):
                for j in range(chip_count):
                    if cost[c][j] <= limit and j not in seen:
                        seen.add(j)
                        if j not in owner or assign(owner[j], seen):
                            owner[j] = c
                            return True
                return False

            if all(assign(c, set()) for c in range(col_count)):
                break
        for j, c in owner.items():
            table[p, c] = j
    return table


def scale_kernel(panel_blocks, slots_ref, rows_ref, factor_ref, out_ref, scaled_ref):
    half = factor_ref.shape[1] // 2
    high, low = split(factor_ref[...])
    rows = rows_ref[...]
    scaled_ref[...] = dot(rows, high) + dot(rows, low)
    out_ref[...] = jnp.zeros_like(out_ref)
    slot_count = slots_ref.shape[0]
    height = rows_ref.shape[0] // slot_count
    for s in range(slot_count):
        block = slots_ref[s]

        @pl.when(block >= 0)
        def _():
            panel = block // panel_blocks
            number = (block - panel * panel_blocks + 1).astype(F32)
            for k in range(2):
                part = scaled_ref[s * height : (s + 1) * height, k * half : (k + 1) * half]
                out_ref[2 * panel + k, :, :half] = part.astype(BF16)
                out_ref[2 * panel + k, :, half:] = jnp.full((height, TAG), number, F32).astype(BF16)


def place_kernel(taken_ref, out_ref):
    width = taken_ref.shape[2] - TAG
    sources = range(taken_ref.shape[0])
    for lanes in range(0, width, TAG):
        totals = [jnp.zeros((taken_ref.shape[1], TAG), F32) for _ in range(out_ref.shape[0])]
        for s in sources:
            tag = taken_ref[s, :, width:].astype(F32)
            value = taken_ref[s, :, lanes : lanes + TAG].astype(F32)
            totals = [t + jnp.where(tag == n + 1, value, 0.0) for n, t in enumerate(totals)]
        for n, total in enumerate(totals):
            out_ref[n, :, lanes : lanes + TAG] = total.astype(BF16)


def turn_kernel(halves_ref, out_ref, rows_ref):
    _, chunks, blocks, height, half = halves_ref.shape
    for k in range(2):
        for c in range(chunks):
            for b in range(blocks):
                first = (b * chunks + c) * height
                rows_ref[first : first + height, :] = halves_ref[k, c, b].astype(F32)
        out_ref[k * half : (k + 1) * half, :] = rows_ref[...].T.astype(BF16)


def product_kernel(col_ref, chip_ref, *refs):
    *tile_refs, parts_ref, factor_ref, out_ref, panel_ref, high_ref, low_ref, sent_ref = refs
    chunks, blocks, height, half = parts_ref.shape
    for b, ref in enumerate(tile_refs):
        rows = ref.shape[1]
        for k in range(2):
            first = (k * len(tile_refs) + b) * rows
            high_ref[first : first + rows, :], low_ref[first : first + rows, :] = split(ref[k])
    for c in range(chunks):
        for b in range(blocks):
            first = (b * chunks + c) * height
            panel_ref[first : first + height, :] = parts_ref[chip_ref[col_ref[0] * chunks + c], b].astype(F32)
    panel = panel_ref[...].astype(BF16)
    sums = dot(high_ref[...], panel) + dot(low_ref[...], panel)
    gram = dot(factor_ref[...], sums.astype(BF16))
    rows = gram.shape[0] // chunks
    share = sums.shape[0] // 2 // chunks
    sent_ref[:, :rows, :] = gram.reshape(chunks, rows, half)
    sums = sums.reshape(2, chunks, share, half)
    for k in range(2):
        sent_ref[:, rows + k * share : rows + (k + 1) * share, :] = sums[k]
    out_ref[...] = sent_ref[...].astype(BF16)


def total_kernel(arrived_ref, total_ref, copies_ref):
    total = arrived_ref[0].astype(F32)
    for s in range(1, arrived_ref.shape[0]):
        total = total + arrived_ref[s].astype(F32)
    first = copies_ref.shape[1]
    rows = total[:first].astype(BF16)
    for copy in range(copies_ref.shape[0]):
        copies_ref[copy] = rows
    total_ref[...] = total[first:]


def body(front_rows, slot_blocks, inv_factor, ancestor_inv):
    col_count = lax.axis_size("col")
    row_count = lax.axis_size("row")
    chip_count = row_count // 2
    col_index = lax.axis_index("col")
    core = lax.axis_index("row") % 2
    slot_count, chunk_rows, width = front_rows.shape
    half = width // 2
    tile_rows, panel_rows = ancestor_inv.shape
    block_rows = chunk_rows * col_count
    panel_blocks = panel_rows // block_rows
    share = tile_rows // col_count
    diag_width = width // col_count
    same_core = [[2 * j + k for j in range(chip_count)] for k in range(2)]
    core_pairs = [[2 * j, 2 * j + 1] for j in range(chip_count)]
    table = short_routes(chip_count, col_count)
    chip_arg = jnp.asarray(table.reshape(-1))
    col_arg = jnp.reshape(col_index, (1,)).astype(jnp.int32)

    def pair_gather(x):
        return lax.all_gather(x, "row", axis=0, axis_index_groups=core_pairs)

    def over_row(x):
        return lax.all_to_all(x, "row", 0, 0, tiled=True, axis_index_groups=same_core)

    def over_col(x):
        return lax.all_to_all(x, "col", 0, 0, tiled=True)

    factor_cols = lax.dynamic_slice_in_dim(inv_factor, col_index * diag_width, diag_width, 1)
    factor_gram = lax.optimization_barrier(
        lax.dot_general(
            factor_cols,
            inv_factor,
            (((0,), (0,)), ((), ())),
            precision=lax.Precision.HIGHEST,
            preferred_element_type=F32,
        )
    )

    by_panel = pl.pallas_call(
        lambda *refs: scale_kernel(panel_blocks, *refs),
        out_shape=jax.ShapeDtypeStruct((row_count, chunk_rows, half + TAG), BF16),
        in_specs=[SMEM, VMEM, VMEM],
        out_specs=VMEM,
        scratch_shapes=[pltpu.VMEM((slot_count * chunk_rows, width), F32)],
        compiler_params=FETCHING,
    )(
        slot_blocks,
        front_rows.reshape(slot_count * chunk_rows, width),
        inv_factor,
    )
    by_panel, tile = lax.optimization_barrier((by_panel, ancestor_inv))
    tiles = [
        pair_gather(tile[first : first + block_rows])
        for first in range(0, tile_rows - block_rows, block_rows)
    ]
    taken, core, *tiles = lax.optimization_barrier(
        (lax.all_to_all(by_panel, "row", 0, 0, tiled=True), core, *tiles)
    )
    piece = pl.pallas_call(
        place_kernel,
        out_shape=jax.ShapeDtypeStruct((panel_blocks, chunk_rows, half), BF16),
        in_specs=[VMEM],
        out_specs=VMEM,
        compiler_params=PARAMS,
    )(taken)

    route = [
        ((2 * p + k) * col_count + c, (2 * int(table[p, c]) + k) * col_count + p)
        for p in range(col_count)
        for k in range(2)
        for c in range(col_count)
    ]
    piece, tile = lax.optimization_barrier((piece, tile))
    turned = lax.ppermute(piece, ("row", "col"), route)
    factor = over_col(jnp.broadcast_to(piece[None], (col_count, *piece.shape)))
    factor, last_tile = lax.optimization_barrier(
        (factor, pair_gather(tile[tile_rows - block_rows :]))
    )
    tiles.append(last_tile)
    tile_factor = pl.pallas_call(
        turn_kernel,
        out_shape=jax.ShapeDtypeStruct((width, 2 * tile_rows), BF16),
        in_specs=[VMEM],
        out_specs=VMEM,
        scratch_shapes=[pltpu.VMEM((2 * tile_rows, half), F32)],
        compiler_params=PARAMS,
    )(pair_gather(factor))
    parts = over_row(jnp.broadcast_to(turned[None], (chip_count, *turned.shape)))

    sent = (col_count, diag_width + 2 * share, half)
    sent = pl.pallas_call(
        product_kernel,
        out_shape=jax.ShapeDtypeStruct(sent, BF16),
        in_specs=[SMEM, SMEM] + [VMEM] * (len(tiles) + 2),
        out_specs=VMEM,
        scratch_shapes=[
            pltpu.VMEM((panel_rows, half), F32),
            pltpu.VMEM((2 * tile_rows, panel_rows), BF16),
            pltpu.VMEM((2 * tile_rows, panel_rows), BF16),
            pltpu.VMEM(sent, F32),
        ],
        compiler_params=pltpu.CompilerParams(vmem_limit_bytes=50 * 2**20),
    )(col_arg, chip_arg, *tiles, parts, tile_factor)
    totals, copies = pl.pallas_call(
        total_kernel,
        out_shape=(
            jax.ShapeDtypeStruct((2 * share, half), F32),
            jax.ShapeDtypeStruct((chip_count, diag_width, half), BF16),
        ),
        in_specs=[VMEM],
        out_specs=(VMEM, VMEM),
        compiler_params=PARAMS,
    )(over_col(sent))
    halves = pair_gather(totals).reshape(2, 2, share, half)
    product = jnp.where(core == 0, halves[:, 0], halves[:, 1])
    product = jnp.concatenate([product[0], product[1]], 1)
    gram_rows = pair_gather(jnp.sum(over_row(copies).astype(F32), axis=0))
    gram_rows = jnp.concatenate([gram_rows[0], gram_rows[1]], 1)
    return (-product, factor_gram + gram_rows)


def solution(mesh):
    in_specs = (P("row", "col", None), P("row"), P(), P("row", "col"))
    out_specs = (P(("row", "col"), None), P("col", None))
    return jax.shard_map(body, mesh=mesh, in_specs=in_specs, out_specs=out_specs, check_vma=False)
```
